256 devices in a mesh: blk: 16 (over y_hi, x, core), row: 16 (over y_lo, z).
Axes of the slice: x: 4, y: 4 (y_hi: 2, y_lo: 2; y = y_hi * 2 + y_lo), z: 8, core: 2. Of those that a mesh axis runs over, the one named last changes fastest.
Arguments:
- images: float32 [16384, 1152], P(('blk', 'row')), may hold values from -0.2 to 0.2
- texts: float32 [16384, 1152], P(('blk', 'row')), may hold values from -0.2 to 0.2
- scale: float32 [1], replicated, may hold values from 4 to 12
- bias: float32 [1], replicated, may hold values from -3 to -1
Outputs:
- image_grad: float32 [16384, 1152], P(('blk', 'row'))
- text_grad: float32 [16384, 1152], P(('blk', 'row'))
The draws below stay inside these ranges and needn't reach their ends.
All inputs are finite; a program needn't handle non-finite values.
Results may differ from the reference program's by a relative error of at most 0.0053.
Values may be sent and summed in bfloat16 or wider, within the bound.
A program may use at most 64 MiB of HBM per device.

```python
import math
import jax
import jax.numpy as jnp
from jax import lax

D = 1152
PAIRS = 16384


def block_scale(rng, extent, shards, least, top_value):
    def one(position, shards_of):
        heights = jax.random.uniform(jax.random.fold_in(jax.random.fold_in(rng, 6), position), (shards_of,), jnp.float32, least / len(shards), top_value / len(shards))
        return jnp.repeat(jnp.exp(heights), extent[position] // shards_of).reshape((-1,) + (1,) * (len(extent) - position - 1))

    gain = one(*shards[0])
    for cut in shards[1:]:
        gain = gain * one(*cut)
    return gain


def noise(stream_key, extent, scale, reach, cuts=(), kind=jnp.bfloat16):
    entries = scale * jax.random.normal(stream_key, extent, jnp.float32)
    if cuts:
        entries = entries * block_scale(stream_key, extent, cuts, -0.22, 0.18)
    return jnp.clip(entries, -reach, reach).astype(kind)


def setup_inputs(seed: int = 0) -> dict:
    streams_of = jax.random.split(jax.random.key(seed), 5)
    return {
        "images": noise(streams_of[0], (PAIRS, D), 0.03, 0.2, ((0, 256),), jnp.float32),
        "texts": noise(streams_of[1], (PAIRS, D), 0.03, 0.2, ((0, 256),), jnp.float32),
        "scale": jnp.clip(jax.random.uniform(streams_of[2], (1,), jnp.float32, 4.0, 12.0), 4.0, 12.0),
        "bias": jnp.clip(jax.random.uniform(streams_of[3], (1,), jnp.float32, -3.0, -1.0), -3.0, -1.0),
    }


EPS = 1e-06

def normalize(values):
    norm_rows = jnp.sqrt(lax.optimization_barrier(jnp.sum(values * values, axis=1, keepdims=True)) + EPS)
    return (values / norm_rows, norm_rows)

def project_back(grad_hat, unit_rows, norm_rows):
    return (grad_hat - unit_rows * lax.optimization_barrier(jnp.sum(unit_rows * grad_hat, axis=1, keepdims=True))) / norm_rows

def reference(images, texts, scale, bias):
    image_unit, image_norm = normalize(images)
    text_unit, text_norm = normalize(texts)
    image_hat = image_unit.astype(jnp.bfloat16)
    text_hat = text_unit.astype(jnp.bfloat16)
    total = images.shape[0]
    width = images.shape[1]
    block = math.gcd(total, 1024)
    nblock = total // block
    columns = jnp.arange(total, dtype=jnp.int32)

    def block_step(text_acc, block_id):
        start = (block_id * block).astype(jnp.int32)
        rows_here = lax.dynamic_slice_in_dim(image_hat, start, block, 0)
        logits = scale[0] * jnp.dot(rows_here, text_hat.T, preferred_element_type=jnp.float32) + bias[0]
        row_ids = start + jnp.arange(block, dtype=jnp.int32)
        sign = jnp.where(row_ids[:, None] == columns[None, :], 1.0, -1.0).astype(logits.dtype)
        coef = (-scale[0] * sign * jax.nn.sigmoid(-sign * logits)).astype(jnp.bfloat16)
        image_part = jnp.dot(coef, text_hat, preferred_element_type=jnp.float32)
        text_acc = text_acc + jnp.dot(coef.T, rows_here, preferred_element_type=jnp.float32)
        return (text_acc, image_part)
    text_hat_grad, image_parts = lax.scan(block_step, jnp.zeros((total, width), jnp.float32), jnp.arange(nblock, dtype=jnp.int32))
    image_hat_grad = image_parts.reshape(total, width)
    image_grad = project_back(image_hat_grad, image_unit, image_norm)
    text_grad = project_back(text_hat_grad, text_unit, text_norm)
    return (image_grad, text_grad)
```

```python
import jax
import jax.numpy as jnp
from jax import lax
from jax.experimental import pallas as pl
from jax.experimental.pallas import tpu as pltpu
from jax.sharding import PartitionSpec as P

EPS = 1e-06
F32 = jnp.float32
BF16 = jnp.bfloat16
MESH = pl.DeviceIdType.MESH
NT = (((1,), (1,)), ((), ()))
NN = (((1,), (0,)), ((), ()))
TN = (((0,), (0,)), ((), ()))

NX, NY, NZ = 4, 4, 8
ROWS = 64
HALF = 32
QUAR = 16
XP, XM = (1, 0, 0, 0), (-1, 0, 0, 0)
YP, YM = (0, 1, 0, 0), (0, -1, 0, 0)
ZP, ZM = (0, 0, 1, 0), (0, 0, -1, 0)
CORE = (0, 0, 0, 1)
NEIGHBOURS = (XP, XM, YP, YM, ZP, ZM, CORE)

IMAGE_ORDER = (
    (2, 2), (2, 1), (2, 3), (1, 2),
    (3, 2), (2, 0), (0, 2), (1, 1),
    (1, 3), (3, 1), (3, 3), (0, 1),
    (0, 3), (1, 0), (3, 0), (0, 0),
)
IMAGE_ROW = {slot: i * ROWS for i, slot in enumerate(IMAGE_ORDER)}
TEXT_ORDER = (4, 3, 5, 2, 6, 1, 7, 0)
TEXT_ROW = {(dz, dc): (i * 2 + dc) * ROWS for i, dz in enumerate(TEXT_ORDER) for dc in range(2)}
NI = len(IMAGE_ORDER) * ROWS
NTX = len(TEXT_ORDER) * 2 * ROWS
BLOCK = 256
MESSAGES = 160


def position():
    blk = lax.axis_index("blk")
    row = lax.axis_index("row")
    return (blk // 2) % NX, (blk // (2 * NX)) * 2 + row // NZ, row % NZ, blk % 2


def device(here, step):
    x = (here[0] + step[0] + NX) % NX
    y = (here[1] + step[1] + NY) % NY
    z = (here[2] + step[2] + NZ) % NZ
    core = (here[3] + step[3]) % 2
    return (((y // 2) * NX + x) * 2 + core, (y % 2) * NZ + z)


def unit_of(values):
    norm_rows = jnp.sqrt(jnp.sum(values * values, axis=1, keepdims=True) + EPS)
    return values / norm_rows, norm_rows


def project_back(grad_hat, unit_rows, norm_rows):
    return (grad_hat - unit_rows * jnp.sum(unit_rows * grad_hat, axis=1, keepdims=True)) / norm_rows


def kernel(
    images, texts, scale, bias, image_grad, text_grad,
    image_hat, text_hat, image_acc, text_acc, coef, out_stage, in_stage, send_sem, recv_sem,
):
    here = position()
    barrier = pltpu.get_barrier_semaphore()
    for step in NEIGHBOURS:
        pl.semaphore_signal(barrier, inc=1, device_id=device(here, step), device_id_type=MESH)
    scale_value = scale[0]
    bias_value = bias[0]

    own_image = pl.ds(IMAGE_ROW[0, 0], ROWS)
    own_text = pl.ds(TEXT_ROW[0, 0], ROWS)
    image_hat[own_image] = unit_of(images[...])[0].astype(BF16)
    text_hat[own_text] = unit_of(texts[...])[0].astype(BF16)
    pl.semaphore_wait(barrier, len(NEIGHBOURS))

    copies = []
    staged = [0]

    def send(src, dst, step):
        n = len(copies)
        assert n < MESSAGES
        copy = pltpu.make_async_remote_copy(
            src_ref=src, dst_ref=dst, send_sem=send_sem.at[n], recv_sem=recv_sem.at[n],
            device_id=device(here, step), device_id_type=MESH,
        )
        copy.start()
        copies.append(copy)
        return copy

    def wait(*arriving):
        for copy in arriving:
            copy.wait_recv()

    def pass_image(step, slot, start, count):
        to = ((slot[0] - step[0]) % NX, (slot[1] - step[1]) % NY)
        return send(
            image_hat.at[pl.ds(IMAGE_ROW[slot] + start, count)],
            image_hat.at[pl.ds(IMAGE_ROW[to] + start, count)],
            step,
        )

    def pass_text(step, dz, start, count):
        to = ((dz - step[2]) % NZ, step[3])
        return send(
            text_hat.at[pl.ds(TEXT_ROW[dz, 0] + start, count)],
            text_hat.at[pl.ds(TEXT_ROW[to] + start, count)],
            step,
        )

    def both(first, second, slot, start):
        return (pass_image(first, slot, start, HALF), pass_image(second, slot, start, HALF))

    def onward_y(dx, start):
        return (pass_image(YP, (dx, 3), start, QUAR), pass_image(YM, (dx, 1), start + QUAR, QUAR))

    def onward_x(dy, start):
        return (pass_image(XP, (3, dy), start, QUAR), pass_image(XM, (1, dy), start + QUAR, QUAR))

    h1, h2 = 0, HALF
    x1 = both(XP, XM, (0, 0), h1)
    y2 = both(YP, YM, (0, 0), h2)
    za = (pass_text(ZP, 0, 0, HALF), pass_text(ZM, 0, 0, HALF))
    x2 = both(XP, XM, (0, 0), h2)
    y1 = both(YP, YM, (0, 0), h1)
    zb = (pass_text(ZP, 0, HALF, HALF), pass_text(ZM, 0, HALF, HALF))
    last = [pass_text(CORE, 0, 0, ROWS)]

    wait(*x1)
    xf1 = onward_x(0, h1)
    y1_3 = both(YP, YM, (3, 0), h1)
    y1_1 = both(YP, YM, (1, 0), h1)
    wait(*y2)
    yf2 = onward_y(0, h2)
    x2_3 = both(XP, XM, (0, 3), h2)
    x2_1 = both(XP, XM, (0, 1), h2)
    wait(*za)
    za = (pass_text(ZP, 7, 0, HALF), pass_text(ZM, 1, 0, HALF))
    wait(*y1)
    last += onward_y(0, h1)
    wait(*x2)
    last += onward_x(0, h2)
    wait(*zb)
    zb = (pass_text(ZP, 7, HALF, HALF), pass_text(ZM, 1, HALF, HALF))
    last += [pass_text(CORE, 7, 0, ROWS), pass_text(CORE, 1, 0, ROWS)]
    wait(*xf1)
    y1_2 = both(YP, YM, (2, 0), h1)
    wait(*yf2)
    x2_2 = both(XP, XM, (0, 2), h2)
    wait(*za)
    za = (pass_text(ZP, 6, 0, HALF), pass_text(ZM, 2, 0, HALF))
    wait(*y1_3)
    last += onward_y(3, h1)
    wait(*x2_3)
    last += onward_x(3, h2)
    wait(*zb)
    zb = (pass_text(ZP, 6, HALF, HALF), pass_text(ZM, 2, HALF, HALF))
    last += [pass_text(CORE, 6, 0, ROWS), pass_text(CORE, 2, 0, ROWS)]
    wait(*y1_1)
    last += onward_y(1, h1)
    wait(*x2_1)
    last += onward_x(1, h2)
    wait(*za)
    z4 = [pass_text(ZP, 5, 0, HALF)]
    wait(*zb)
    z4 += [pass_text(ZM, 3, HALF, HALF)]
    last += [pass_text(CORE, 5, 0, ROWS), pass_text(CORE, 3, 0, ROWS)]
    wait(*y1_2)
    last += onward_y(2, h1)
    wait(*x2_2)
    last += onward_x(2, h2)
    wait(*z4)
    last += [pass_text(CORE, 4, 0, ROWS)]
    wait(*last)

    for block in range(NI // BLOCK):
        rows = pl.ds(block * BLOCK, BLOCK)
        logits = scale_value * lax.dot_general(image_hat[rows], text_hat[...], NT, preferred_element_type=F32) + bias_value
        coef[rows] = (scale_value * jax.nn.sigmoid(logits)).astype(BF16)
        if block * BLOCK <= IMAGE_ROW[0, 0] < (block + 1) * BLOCK:
            top = IMAGE_ROW[0, 0] - block * BLOCK
            left = TEXT_ROW[0, 0]
            pair = logits[top : top + ROWS, left : left + 2 * ROWS]
            sign = jnp.where(
                lax.broadcasted_iota(jnp.int32, pair.shape, 0) == lax.broadcasted_iota(jnp.int32, pair.shape, 1), 1.0, -1.0
            ).astype(F32)
            coef[own_image, pl.ds(left, 2 * ROWS)] = (-scale_value * sign * jax.nn.sigmoid(-sign * pair)).astype(BF16)

    def image_block(block):
        rows = pl.ds(block * BLOCK, BLOCK)
        image_acc[rows] = lax.dot_general(coef[rows], text_hat[...], NN, preferred_element_type=F32)

    def text_block(start, count):
        rows = pl.ds(start, count)
        text_acc[rows] = lax.dot_general(coef[:, rows], image_hat[...], TN, preferred_element_type=F32)

    def ship(acc, row, to_row, count, step):
        at = staged[0]
        staged[0] += count
        piece = pl.ds(at, count)
        out_stage[piece] = acc[pl.ds(row, count)].astype(BF16)
        return (send(out_stage.at[piece], in_stage.at[piece], step), acc, to_row, count, at)

    def absorb(*messages):
        for copy, acc, row, count, at in messages:
            copy.wait_recv()
            rows = pl.ds(row, count)
            acc[rows] = acc[rows] + in_stage[pl.ds(at, count)].astype(F32)

    def ship_image(step, slot, start, count):
        to = ((slot[0] - step[0]) % NX, (slot[1] - step[1]) % NY)
        return ship(image_acc, IMAGE_ROW[slot] + start, IMAGE_ROW[to] + start, count, step)

    def ship_text(step, dz, start, count):
        to = ((dz - step[2]) % NZ, 0)
        return ship(text_acc, TEXT_ROW[dz, step[3]] + start, TEXT_ROW[to] + start, count, step)

    def far_y(dx, start):
        return (ship_image(YM, (dx, 2), start, QUAR), ship_image(YP, (dx, 2), start + QUAR, QUAR))

    def near_y(dx, start):
        return (ship_image(YM, (dx, 3), start, HALF), ship_image(YP, (dx, 1), start, HALF))

    def far_x(dy, start):
        return (ship_image(XM, (2, dy), start, QUAR), ship_image(XP, (2, dy), start + QUAR, QUAR))

    def near_x(dy, start):
        return (ship_image(XM, (3, dy), start, HALF), ship_image(XP, (1, dy), start, HALF))

    fy, fx, ny, nx = {}, {}, {}, {}
    text_block(0, 512)
    c4, c3, c5, c2 = [ship_text(CORE, dz, 0, ROWS) for dz in (4, 3, 5, 2)]
    image_block(0)
    fy[2], fx[2] = far_y(2, h1), far_x(2, h2)
    fy[1], fx[1] = far_y(1, h1), far_x(1, h2)
    fx[3] = far_x(3, h2)
    absorb(c4, c3, c5)
    za, zb = ship_text(ZP, 4, 0, HALF), ship_text(ZM, 4, HALF, HALF)
    zc, zd = ship_text(ZP, 3, HALF, HALF), ship_text(ZM, 5, 0, HALF)
    image_block(1)
    fy[3], fy[0] = far_y(3, h1), far_y(0, h1)
    fx[0] = far_x(0, h2)
    text_block(512, 512)
    c6, c1, c7, c0 = [ship_text(CORE, dz, 0, ROWS) for dz in (6, 1, 7, 0)]
    absorb(*fy[2])
    ny[2] = near_y(2, h1)
    absorb(*fx[2])
    nx[2] = near_x(2, h2)
    image_block(2)
    absorb(za, zb)
    za, zb = ship_text(ZP, 3, 0, HALF), ship_text(ZM, 5, HALF, HALF)
    absorb(*fx[1])
    nx[1] = near_x(1, h2)
    absorb(*fy[1])
    ny[1] = near_y(1, h1)
    image_block(3)
    absorb(*fx[3])
    nx[3] = near_x(3, h2)
    absorb(*fy[3])
    ny[3] = near_y(3, h1)
    absorb(c2, c6)
    absorb(zc, zd)
    zc, zd = ship_text(ZP, 2, HALF, HALF), ship_text(ZM, 6, 0, HALF)
    absorb(*fy[0])
    ny[0] = near_y(0, h1)
    absorb(*fx[0])
    nx[0] = near_x(0, h2)
    absorb(za, zb)
    za, zb = ship_text(ZP, 2, 0, HALF), ship_text(ZM, 6, HALF, HALF)
    absorb(*ny[2])
    gx = far_x(0, h1)
    absorb(*nx[2])
    gy = far_y(0, h2)
    absorb(c1, c7)
    absorb(zc, zd)
    zc, zd = ship_text(ZP, 1, HALF, HALF), ship_text(ZM, 7, 0, HALF)
    absorb(*ny[1], *ny[3])
    absorb(*nx[1], *nx[3])
    absorb(*gx)
    kx = near_x(0, h1)
    absorb(*gy)
    ky = near_y(0, h2)
    absorb(za, zb)
    za, zb = ship_text(ZP, 1, 0, HALF), ship_text(ZM, 7, HALF, HALF)
    absorb(c0)
    absorb(*ny[0])
    absorb(*nx[0])
    absorb(*kx, *ky)
    image_unit, image_norm = unit_of(images[...])
    image_grad[...] = project_back(image_acc[own_image], image_unit, image_norm)
    absorb(zc, zd, za, zb)
    text_unit, text_norm = unit_of(texts[...])
    text_grad[...] = project_back(text_acc[own_text], text_unit, text_norm)
    for copy in copies:
        copy.wait_send()


def body(images, texts, scale, bias):
    width = images.shape[1]
    vmem = pl.BlockSpec(memory_space=pltpu.VMEM)
    smem = pl.BlockSpec(memory_space=pltpu.SMEM)
    shard = jax.ShapeDtypeStruct(images.shape, F32)
    return pl.pallas_call(
        kernel,
        out_shape=(shard, shard),
        in_specs=[vmem, vmem, smem, smem],
        out_specs=(vmem, vmem),
        scratch_shapes=[
            pltpu.VMEM((NI, width), BF16),
            pltpu.VMEM((NTX, width), BF16),
            pltpu.VMEM((NI, width), F32),
            pltpu.VMEM((NTX, width), F32),
            pltpu.VMEM((NI, NTX), BF16),
            pltpu.VMEM((2048, width), BF16),
            pltpu.VMEM((2048, width), BF16),
            pltpu.SemaphoreType.DMA((MESSAGES,)),
            pltpu.SemaphoreType.DMA((MESSAGES,)),
        ],
        compiler_params=pltpu.CompilerParams(
            collective_id=0, has_side_effects=True, vmem_limit_bytes=48 * 2**20
        ),
    )(images, texts, scale, bias)


def solution(mesh):
    placed = (P(("blk", "row"), None), P(("blk", "row"), None), P(), P())
    return jax.shard_map(
        body,
        mesh=mesh,
        in_specs=placed,
        out_specs=(P(("blk", "row"), None), P(("blk", "row"), None)),
        check_vma=False,
    )
```

```python
import jax
import jax.numpy as jnp
from jax import lax
from jax.experimental import pallas as pl
from jax.experimental.pallas import tpu as pltpu
from jax.sharding import PartitionSpec as P

EPS = 1e-06
F32 = jnp.float32
BF16 = jnp.bfloat16
MESH = pl.DeviceIdType.MESH
NT = (((1,), (1,)), ((), ()))
NN = (((1,), (0,)), ((), ()))
TN = (((0,), (0,)), ((), ()))

NX, NY, NZ = 4, 4, 8
ROWS = 64
HALF = 32
QUAR = 16
BLOCK = 256
LANES = 128
XP, XM = (1, 0, 0, 0), (-1, 0, 0, 0)
YP, YM = (0, 1, 0, 0), (0, -1, 0, 0)
ZP, ZM, ZP2, ZM2 = (0, 0, 1, 0), (0, 0, -1, 0), (0, 0, 2, 0), (0, 0, -2, 0)
CORE = (0, 0, 0, 1)
PARTNERS = (XP, XM, YP, YM, ZP, ZM, ZP2, ZM2, CORE)

IMAGE_ORDER = (
    (2, 2), (1, 2), (3, 2), (2, 1),
    (2, 3), (2, 0), (0, 2), (1, 1),
    (3, 1), (1, 3), (3, 3), (0, 1),
    (0, 3), (1, 0), (3, 0), (0, 0),
)
IMAGE_ROW = {slot: i * ROWS for i, slot in enumerate(IMAGE_ORDER)}
TEXT_ORDER = (4, 3, 5, 2, 6, 1, 7, 0)
NI = len(IMAGE_ORDER) * ROWS
NTH = len(TEXT_ORDER) * ROWS
NTX = 2 * NTH
TEXT_ROW = {(dz, dc): dc * NTH + i * ROWS for i, dz in enumerate(TEXT_ORDER) for dc in range(2)}
OWN_HI, OWN_LO, OTHER_HI, OTHER_LO = 0, BLOCK, NTH, NTH + BLOCK
OWN_IMAGE, OWN_TEXT = IMAGE_ROW[0, 0], TEXT_ROW[0, 0]
STAGE = 2176
GROUPS = 64
(
    X1, X2, Y1, Y2, XD, YD, Y1_1, Y1_2, Y1_3, X2_1, X2_2, X2_3, LY0, LY1, LY2, LY3, LX0, LX1, LX2,
    LX3, ZA0, ZA1, ZA2, ZB0, ZB1, ZB2, ZC, ZD, T0, T1, T2, T3, T4, COH0, COH1, COH2, COH3, COL0, COL1,
    COL2, COL3, CPH0, CPH1, CPH2, CPH3, CPL0, CPL1, CPL2, CPL3, I0, I1, I2, I3, OH, OL, PH, PL, S0,
    S1, FX0, FX1, FX2, FX3, FY0, FY1, FY2, FY3, NX0, NX1, NX2, NX3, NY0, NY1, NY2, NY3, GX, GY, KX,
    KY, RA1, RA2, RA3, RB1, RB2, RB3, RC, RD, END_IMAGE, END_TEXT, LA, LB, Z4,
) = range(92)
Y1S, X2S = (Y1, Y1_1, Y1_2, Y1_3), (X2, X2_1, X2_2, X2_3)
LX, LY, I = (LX0, LX1, LX2, LX3), (LY0, LY1, LY2, LY3), (I0, I1, I2, I3)
FX, FY, NX_, NY_ = (FX0, FX1, FX2, FX3), (FY0, FY1, FY2, FY3), (NX0, NX1, NX2, NX3), (NY0, NY1, NY2, NY3)
COH, COL = (COH0, COH1, COH2, COH3), (COL0, COL1, COL2, COL3)
CPH, CPL = (CPH0, CPH1, CPH2, CPH3), (CPL0, CPL1, CPL2, CPL3)

ORDER = (
    ZA0, X1, Y2, ZB0, X2, Y1, Y1_1, ZA1, XD, X2_3, T0, YD, X2_1, Y1_3, ZB1, ZA2, T1, Y1_2, X2_2, T2, ZB2,
    LY0, COL3, ZD, LX0, ZC, LX3, LY3, LY1, COL2, LX1, CPL3, LX2, LY2, T3, COL1, CPL2, CPL1, T4, COH2,
    CPH0, CPH2, COL0, CPH3, CPH1, CPL0, COH0, I0, COH3, PH, S0, FY3, FX2, FY2, COH1, I1, OH, RD, RC, FY1,
    FX1, FX3, NX2, RB3, NY2, FY0, I2, PL, S1, FX0, NY1, RA3, NX1, OL, NY3, RB2, GX, NX3, GY, RA2, I3, NX0,
    NY0, RB1, KX, KY, RA1, END_IMAGE, END_TEXT,
)


class Plan:
    def __init__(self, run):
        self.run = run
        self.parts = {}
        self.coming = {}
        self.taken = set()
        self.staged = NTH
        self.steps = {}
        self.gather()
        self.compute()
        self.reduce()

    def add(self, name, after, needs, *actions):
        self.steps[name] = (after, needs, actions)

    def execute(self, order):
        done = set()
        for name in order:
            after, needs, actions = self.steps[name]
            assert done.issuperset(needs)
            self.take(after)
            for action, *args in actions:
                action(*args)
            done.add(name)

    def take(self, names):
        for name in names:
            if name not in self.taken:
                self.taken.add(name)
                self.run.wait(name)
                for key, start, count, at in self.coming.get(name, ()):
                    self.parts.setdefault(key, []).append((start, count, at))

    def pass_image(self, name, step, slot, start, count):
        to = ((slot[0] - step[0]) % NX, (slot[1] - step[1]) % NY)
        self.run.copy(name, 0, "image", IMAGE_ROW[slot] + start, "image", IMAGE_ROW[to] + start, count, step)

    def pass_text(self, name, step, dz, start, count):
        to = (dz - step[2]) % NZ
        self.run.copy(name, 0, "text", TEXT_ROW[dz, 0] + start, "text", TEXT_ROW[to, 0] + start, count, step)

    def share(self, name, dz, slots):
        self.run.copy(name, 0, "text", TEXT_ROW[dz, 0], "text", TEXT_ROW[dz, 1], slots * ROWS, CORE)

    def both_x(self, name, dy, start):
        self.pass_image(name, XP, (0, dy), start, HALF)
        self.pass_image(name, XM, (0, dy), start, HALF)

    def both_y(self, name, dx, start):
        self.pass_image(name, YP, (dx, 0), start, HALF)
        self.pass_image(name, YM, (dx, 0), start, HALF)

    def onward_x(self, name, dy, start):
        self.pass_image(name, XP, (3, dy), start, QUAR)
        self.pass_image(name, XM, (1, dy), start + QUAR, QUAR)

    def onward_y(self, name, dx, start):
        self.pass_image(name, YP, (dx, 3), start, QUAR)
        self.pass_image(name, YM, (dx, 1), start + QUAR, QUAR)

    def ring(self, name, up, down, start):
        self.pass_text(name, ZP, up, start, HALF)
        self.pass_text(name, ZM, down, start, HALF)

    def gather(self):
        add, h1, h2 = self.add, 0, HALF
        add(X1, (), (), (self.both_x, X1, 0, h1))
        add(X2, (), (), (self.both_x, X2, 0, h2))
        add(Y1, (), (), (self.both_y, Y1, 0, h1))
        add(Y2, (), (), (self.both_y, Y2, 0, h2))
        add(XD, (X1,), (), (self.onward_x, XD, 0, h1))
        add(YD, (Y2,), (), (self.onward_y, YD, 0, h2))
        for d, far, near in ((3, X1, Y2), (1, X1, Y2), (2, XD, YD)):
            add(Y1S[d], (far,), (), (self.both_y, Y1S[d], d, h1))
            add(X2S[d], (near,), (), (self.both_x, X2S[d], d, h2))
        for d, group in enumerate((LA, LB, LB, LA)):
            add(LY[d], (Y1S[d],), (), (self.onward_y, group, d, h1))
            add(LX[d], (X2S[d],), (), (self.onward_x, group, d, h2))
        add(ZA0, (), (), (self.ring, ZA0, 0, 0, 0))
        add(ZB0, (), (), (self.ring, ZB0, 0, 0, HALF))
        add(ZA1, (ZA0,), (), (self.ring, ZA1, 7, 1, 0))
        add(ZB1, (ZB0,), (), (self.ring, ZB1, 7, 1, HALF))
        add(ZA2, (ZA1,), (), (self.ring, ZA2, 6, 2, 0))
        add(ZB2, (ZB1,), (), (self.ring, ZB2, 6, 2, HALF))
        add(ZC, (ZA1,), (), (self.pass_text, Z4, ZP2, 6, 0, HALF))
        add(ZD, (ZB1,), (), (self.pass_text, Z4, ZM2, 2, HALF, HALF))
        add(T0, (), (), (self.share, T0, 0, 1))
        add(T1, (ZA0, ZB0), (), (self.share, T1, 1, 2))
        add(T2, (ZA1, ZB1), (), (self.share, T2, 2, 2))
        add(T3, (ZA2, ZB2), (), (self.share, T3, 3, 2))
        add(T4, (Z4,), (ZC, ZD), (self.share, T4, 4, 1))

    def compute(self):
        run = self.run
        images = (
            (LA, LB, X2_2, Y1_2),
            (Y1_2, XD, YD, LA, Y1_1, X2_1),
            (Y1_3, Y1_1, X2_1, X2_3, Y1, Y2),
            (X1, X2, Y1, Y2),
        )
        texts = (
            (OH, COH, OWN_HI, (ZA1, ZB1, ZA2, ZB2, Z4)),
            (OL, COL, OWN_LO, (ZA0, ZB0, ZA1, ZB1)),
            (PH, CPH, OTHER_HI, (T2, T3, T4)),
            (PL, CPL, OTHER_LO, (T0, T1, T2)),
        )
        sent = {LA: (LY0, LX0, LY3, LX3), LB: (LY1, LX1, LY2, LX2), Z4: (ZC, ZD)}
        for block, here in enumerate(images):
            for _, coefs, start, there in texts:
                waits = here + there
                needs = sum((sent.get(wait, (wait,)) for wait in waits), ())
                self.add(coefs[block], waits, needs, (run.coef, block, start))
        for block in range(4):
            self.add(I[block], (), (COH[block], COL[block], CPH[block], CPL[block]), (run.images, block))
        for name, coefs, start, _ in texts:
            self.add(name, (), coefs, (run.texts, start))

    def ship(self, name, key, to_key, start, count, step):
        at = self.staged
        self.staged += count
        self.run.stage(key[0], self.row(key), self.parts.get(key, ()), start, count, at)
        self.run.copy(name, 1, "out", at, "in", at, count, step)
        self.coming.setdefault(name, []).append((to_key, start, count, at))

    def row(self, key):
        return IMAGE_ROW[key[1]] if key[0] == "image" else TEXT_ROW[key[1]]

    def ship_image(self, name, step, slot, start, count):
        to = ((slot[0] - step[0]) % NX, (slot[1] - step[1]) % NY)
        self.ship(name, ("image", slot), ("image", to), start, count, step)

    def ship_text(self, name, step, dz, start, count):
        self.ship(name, ("text", (dz, 0)), ("text", ((dz - step[2]) % NZ, 0)), start, count, step)

    def swap(self, name, first, slots):
        start, count = TEXT_ROW[first, 1], slots * ROWS
        at = start - NTH
        self.run.stage("text", start, (), 0, count, at)
        self.run.copy(name, 1, "out", at, "in", at, count, CORE)
        self.coming[name] = [
            (("text", (dz, 0)), 0, ROWS, TEXT_ROW[dz, 0]) for dz in TEXT_ORDER if at <= TEXT_ROW[dz, 0] < at + count
        ]

    def far_x(self, name, dy, start):
        self.ship_image(name, XM, (2, dy), start, QUAR)
        self.ship_image(name, XP, (2, dy), start + QUAR, QUAR)

    def far_y(self, name, dx, start):
        self.ship_image(name, YM, (dx, 2), start, QUAR)
        self.ship_image(name, YP, (dx, 2), start + QUAR, QUAR)

    def near_x(self, name, dy, start):
        self.ship_image(name, XM, (3, dy), start, HALF)
        self.ship_image(name, XP, (1, dy), start, HALF)

    def near_y(self, name, dx, start):
        self.ship_image(name, YM, (dx, 3), start, HALF)
        self.ship_image(name, YP, (dx, 1), start, HALF)

    def ring_back(self, name, up, down, start):
        self.ship_text(name, ZP, up, start, HALF)
        self.ship_text(name, ZM, down, start, HALF)

    def reduce(self):
        add, run, h1, h2 = self.add, self.run, 0, HALF

        def blocks(*slots):
            return tuple(sorted({I[IMAGE_ROW[slot] // BLOCK] for slot in slots}))

        for d in range(4):
            add(FY[d], (), blocks((d, 2)), (self.far_y, FY[d], d, h1))
            add(FX[d], (), blocks((2, d)), (self.far_x, FX[d], d, h2))
            add(NY_[d], (FY[d],), (FY[d],) + blocks((d, 3), (d, 1)), (self.near_y, NY_[d], d, h1))
            add(NX_[d], (FX[d],), (FX[d],) + blocks((3, d), (1, d)), (self.near_x, NX_[d], d, h2))
        add(GX, (NY2,), (NY2,) + blocks((2, 0)), (self.far_x, GX, 0, h1))
        add(GY, (NX2,), (NX2,) + blocks((0, 2)), (self.far_y, GY, 0, h2))
        add(KX, (NY1, NY3, GX), (NY1, NY3, GX) + blocks((3, 0), (1, 0)), (self.near_x, KX, 0, h1))
        add(KY, (NX1, NX3, GY), (NX1, NX3, GY) + blocks((0, 3), (0, 1)), (self.near_y, KY, 0, h2))
        add(S0, (), (PH,), (self.swap, S0, 4, 4))
        add(S1, (), (PL,), (self.swap, S1, 6, 4))
        add(RC, (S0,), (S0, OH), (self.ship_text, RC, ZP2, 4, 0, HALF))
        add(RD, (S0,), (S0, OH), (self.ship_text, RD, ZM2, 4, HALF, HALF))
        add(RA3, (S0,), (S0, OH), (self.ring_back, RA3, 3, 5, 0))
        add(RB3, (S0,), (S0, OH), (self.ring_back, RB3, 3, 5, HALF))
        add(RA2, (S0, S1, RC, RA3), (S1, RC, RA3, OL), (self.ring_back, RA2, 2, 6, 0))
        add(RB2, (S0, S1, RD, RB3), (S1, RD, RB3, OL), (self.ring_back, RB2, 2, 6, HALF))
        add(RA1, (RA2,), (RA2,), (self.ring_back, RA1, 1, 7, 0))
        add(RB1, (RB2,), (RB2,), (self.ring_back, RB1, 1, 7, HALF))
        add(END_IMAGE, (KX, KY, NY0, NX0), (KX, KY, NY0, NX0, I3), (self.finish, "image", (0, 0)))
        add(END_TEXT, (RA1, RB1), (RA1, RB1), (self.finish, "text", (0, 0)))

    def finish(self, kind, slot):
        self.run.finish(kind, self.row((kind, slot)), self.parts[kind, slot])


def position():
    blk = lax.axis_index("blk")
    row = lax.axis_index("row")
    return (blk // 2) % NX, (blk // (2 * NX)) * 2 + row // NZ, row % NZ, blk % 2


def device(here, step):
    x = (here[0] + step[0] + NX) % NX
    y = (here[1] + step[1] + NY) % NY
    z = (here[2] + step[2] + NZ) % NZ
    core = (here[3] + step[3]) % 2
    return (((y // 2) * NX + x) * 2 + core, (y % 2) * NZ + z)


def unit_of(values):
    norm_rows = jnp.sqrt(jnp.sum(values * values, axis=1, keepdims=True) + EPS)
    return values / norm_rows, norm_rows


def project_back(grad_hat, unit_rows, norm_rows):
    return (grad_hat - unit_rows * jnp.sum(unit_rows * grad_hat, axis=1, keepdims=True)) / norm_rows


def kernel(
    images, texts, scale, bias, image_hat_grad, text_hat_grad,
    image_hat, text_hat, image_acc, text_acc, coef, out_stage, in_stage, send_sem, recv_sem,
):
    here = position()
    barrier = pltpu.get_barrier_semaphore()
    for step in PARTNERS:
        pl.semaphore_signal(barrier, inc=1, device_id=device(here, step), device_id_type=MESH)
    scale_value = scale[0]
    bias_value = bias[0]
    buffers = {"image": image_hat, "text": text_hat, "out": out_stage, "in": in_stage}
    sums = {"image": image_acc, "text": text_acc}
    grads = {"image": image_hat_grad, "text": text_hat_grad}

    class Run:
        def __init__(self):
            self.rows = {}
            self.index = {}
            self.sent = [0, 0]

        def copy(self, name, phase, source, row, target, to_row, count, step):
            self.rows[name] = self.rows.get(name, 0) + count
            self.sent[phase] += count
            pltpu.make_async_remote_copy(
                src_ref=buffers[source].at[pl.ds(row, count)],
                dst_ref=buffers[target].at[pl.ds(to_row, count)],
                send_sem=send_sem.at[phase],
                recv_sem=recv_sem.at[self.index.setdefault(name, len(self.index))],
                device_id=device(here, step),
                device_id_type=MESH,
            ).start()

        def whole(self, rows, phase, name):
            return pltpu.make_async_remote_copy(
                src_ref=out_stage.at[pl.ds(0, rows)],
                dst_ref=in_stage.at[pl.ds(0, rows)],
                send_sem=send_sem.at[phase],
                recv_sem=recv_sem.at[self.index[name]],
                device_id=device(here, CORE),
                device_id_type=MESH,
            )

        def wait(self, *names):
            for name in names:
                self.whole(self.rows[name], 0, name).wait_recv()

        def wait_sent(self):
            for phase, rows in enumerate(self.sent):
                if rows:
                    self.whole(rows, phase, X1).wait_send()

        def coef(self, block, start):
            rows, cols = pl.ds(block * BLOCK, BLOCK), pl.ds(start, BLOCK)
            dots = lax.dot_general(image_hat[rows], text_hat[cols], NT, preferred_element_type=F32)
            logits = scale_value * dots + bias_value
            coef[rows, cols] = (scale_value * jax.nn.sigmoid(logits)).astype(BF16)
            top, left = OWN_IMAGE - block * BLOCK, OWN_TEXT - start
            if 0 <= top < BLOCK and 0 <= left < BLOCK:
                base = left // LANES * LANES
                pairs = logits[top : top + ROWS, base : base + LANES]
                row = lax.broadcasted_iota(jnp.int32, pairs.shape, 0)
                col = lax.broadcasted_iota(jnp.int32, pairs.shape, 1)
                sign = jnp.where(col - row == left - base, 1.0, -1.0).astype(F32)
                coef[pl.ds(OWN_IMAGE, ROWS), pl.ds(start + base, LANES)] = (
                    -scale_value * sign * jax.nn.sigmoid(-sign * pairs)
                ).astype(BF16)

        def images(self, block):
            rows = pl.ds(block * BLOCK, BLOCK)
            image_acc[rows] = lax.dot_general(coef[rows], text_hat[...], NN, preferred_element_type=F32)

        def texts(self, start):
            rows = pl.ds(start, BLOCK)
            text_acc[rows] = lax.dot_general(coef[:, rows], image_hat[...], TN, preferred_element_type=F32)

        def total(self, kind, row, parts, first, count):
            value = sums[kind][pl.ds(row + first, count)]
            for begin, size, at in parts:
                if begin <= first and first + count <= begin + size:
                    value = value + in_stage[pl.ds(at + first - begin, count)].astype(F32)
            return value

        def stage(self, kind, row, parts, start, count, at):
            step = QUAR if parts else min(count, ROWS)
            for first in range(start, start + count, step):
                value = self.total(kind, row, parts, first, step)
                out_stage[pl.ds(at + first - start, step)] = value.astype(BF16)

        def finish(self, kind, row, parts):
            for first in (0, HALF):
                grads[kind][pl.ds(first, HALF)] = self.total(kind, row, parts, first, HALF)

    run = Run()
    plan = Plan(run)
    image_hat[pl.ds(OWN_IMAGE, ROWS)] = unit_of(images[...])[0].astype(BF16)
    text_hat[pl.ds(OWN_TEXT, ROWS)] = unit_of(texts[...])[0].astype(BF16)
    pl.semaphore_wait(barrier, len(PARTNERS))
    plan.execute(ORDER)
    run.wait_sent()


def body(images, texts, scale, bias):
    width = images.shape[1]
    vmem = pl.BlockSpec(memory_space=pltpu.VMEM)
    smem = pl.BlockSpec(memory_space=pltpu.SMEM)
    shard = jax.ShapeDtypeStruct(images.shape, F32)
    image_hat_grad, text_hat_grad = pl.pallas_call(
        kernel,
        out_shape=(shard, shard),
        in_specs=[vmem, vmem, smem, smem],
        out_specs=(vmem, vmem),
        scratch_shapes=[
            pltpu.VMEM((NI, width), BF16),
            pltpu.VMEM((NTX, width), BF16),
            pltpu.VMEM((NI, width), F32),
            pltpu.VMEM((NTX, width), F32),
            pltpu.VMEM((NI, NTX), BF16),
            pltpu.VMEM((STAGE, width), BF16),
            pltpu.VMEM((STAGE, width), BF16),
            pltpu.SemaphoreType.DMA((2,)),
            pltpu.SemaphoreType.DMA((GROUPS,)),
        ],
        compiler_params=pltpu.CompilerParams(
            collective_id=0, has_side_effects=True, vmem_limit_bytes=48 * 2**20
        ),
    )(images, texts, scale, bias)
    return project_back(image_hat_grad, *unit_of(images)), project_back(text_hat_grad, *unit_of(texts))


def solution(mesh):
    placed = (P(("blk", "row"), None), P(("blk", "row"), None), P(), P())
    return jax.shard_map(
        body,
        mesh=mesh,
        in_specs=placed,
        out_specs=(P(("blk", "row"), None), P(("blk", "row"), None)),
        check_vma=False,
    )
```

```python
import jax
import jax.numpy as jnp
from jax import lax
from jax.experimental import pallas as pl
from jax.experimental.pallas import tpu as pltpu
from jax.sharding import PartitionSpec as P

EPS = 1e-06
F32 = jnp.float32
BF16 = jnp.bfloat16
MESH = pl.DeviceIdType.MESH
NT = (((1,), (1,)), ((), ()))
NN = (((1,), (0,)), ((), ()))
TN = (((0,), (0,)), ((), ()))

NX, NY, NZ = 4, 4, 8
ROWS = 64
HALF = 32
QUAR = 16
BLOCK = 256
LANES = 128
XP, XM = (1, 0, 0, 0), (-1, 0, 0, 0)
YP, YM = (0, 1, 0, 0), (0, -1, 0, 0)
ZP, ZM, ZP2, ZM2 = (0, 0, 1, 0), (0, 0, -1, 0), (0, 0, 2, 0), (0, 0, -2, 0)
CORE = (0, 0, 0, 1)
PARTNERS = (XP, XM, YP, YM, ZP, ZM, ZP2, ZM2, CORE)

IMAGE_ORDER = (
    (2, 2), (1, 2), (3, 2), (2, 1),
    (2, 3), (2, 0), (0, 2), (1, 1),
    (3, 1), (1, 3), (3, 3), (0, 1),
    (0, 3), (1, 0), (3, 0), (0, 0),
)
IMAGE_ROW = {slot: i * ROWS for i, slot in enumerate(IMAGE_ORDER)}
TEXT_ORDER = (4, 3, 5, 2, 6, 1, 7, 0)
NI = len(IMAGE_ORDER) * ROWS
NTH = len(TEXT_ORDER) * ROWS
NTX = 2 * NTH
TEXT_ROW = {(dz, dc): dc * NTH + i * ROWS for i, dz in enumerate(TEXT_ORDER) for dc in range(2)}
OWN_HI, OWN_LO, OTHER_HI, OTHER_LO = 0, BLOCK, NTH, NTH + BLOCK
OWN_IMAGE, OWN_TEXT = IMAGE_ROW[0, 0], TEXT_ROW[0, 0]
STAGE = 2176
GROUPS = 64
(
    X1, X2, Y1, Y2, XD, YD, Y1_1, Y1_2, Y1_3, X2_1, X2_2, X2_3, LY0, LY1, LY2, LY3, LX0, LX1, LX2,
    LX3, ZA0, ZA1, ZA2, ZB0, ZB1, ZB2, ZC, ZD, T0, T1, T2, T3, T4, COH0, COH1, COH2, COH3, COL0, COL1,
    COL2, COL3, CPH0, CPH1, CPH2, CPH3, CPL0, CPL1, CPL2, CPL3, I0, I1, I2, I3, OH, OL, PH, PL, S0,
    S1, FX0, FX1, FX2, FX3, FY0, FY1, FY2, FY3, NX0, NX1, NX2, NX3, NY0, NY1, NY2, NY3, GX, GY, KX,
    KY, RA1, RA2, RA3, RB1, RB2, RB3, RC, RD, END_IMAGE, END_TEXT, LA, LB, Z4,
) = range(92)
Y1S, X2S = (Y1, Y1_1, Y1_2, Y1_3), (X2, X2_1, X2_2, X2_3)
LX, LY, I = (LX0, LX1, LX2, LX3), (LY0, LY1, LY2, LY3), (I0, I1, I2, I3)
FX, FY, NX_, NY_ = (FX0, FX1, FX2, FX3), (FY0, FY1, FY2, FY3), (NX0, NX1, NX2, NX3), (NY0, NY1, NY2, NY3)
COH, COL = (COH0, COH1, COH2, COH3), (COL0, COL1, COL2, COL3)
CPH, CPL = (CPH0, CPH1, CPH2, CPH3), (CPL0, CPL1, CPL2, CPL3)

ORDER = (
    Y2, X1, ZB0, X2, ZA0, Y1, X2_3, ZB1, Y1_1, YD, XD, Y1_3, ZA1, X2_1, T1, Y1_2, ZB2, X2_2, T0, LY0, LX0,
    ZD, LX3, LY1, T2, ZC, LY3, COL2, CPL3, CPL2, ZA2, LX1, LY2, LX2, COL1, CPL1, T4, COL3, T3, COH2, COH3,
    COH1, COH0, CPL0, CPH2, CPH0, CPH3, CPH1, PH, S0, COL0, OH, I0, RD, RB3, FY2, RC, FX2, I1, FY3, FX1,
    PL, FX3, FY1, S1, NY2, NX2, I2, RA3, FY0, NX1, I3, FX0, NY1, OL, RB2, NX3, GX, GY, NY3, RA2, NX0, NY0,
    RB1, KY, KX, RA1, END_IMAGE, END_TEXT,
)


class Plan:
    def __init__(self, run):
        self.run = run
        self.parts = {}
        self.coming = {}
        self.taken = set()
        self.staged = NTH
        self.steps = {}
        self.gather()
        self.compute()
        self.reduce()

    def add(self, name, after, needs, *actions):
        self.steps[name] = (after, needs, actions)

    def execute(self, order):
        done = set()
        for name in order:
            after, needs, actions = self.steps[name]
            assert done.issuperset(needs)
            self.take(after)
            for action, *args in actions:
                action(*args)
            done.add(name)

    def take(self, names):
        for name in names:
            if name not in self.taken:
                self.taken.add(name)
                self.run.wait(name)
                for key, start, count, at in self.coming.get(name, ()):
                    self.parts.setdefault(key, []).append((start, count, at))

    def pass_image(self, name, step, slot, start, count):
        to = ((slot[0] - step[0]) % NX, (slot[1] - step[1]) % NY)
        self.run.copy(name, 0, "image", IMAGE_ROW[slot] + start, "image", IMAGE_ROW[to] + start, count, step)

    def pass_text(self, name, step, dz, start, count):
        to = (dz - step[2]) % NZ
        self.run.copy(name, 0, "text", TEXT_ROW[dz, 0] + start, "text", TEXT_ROW[to, 0] + start, count, step)

    def share(self, name, dz, slots):
        self.run.copy(name, 0, "text", TEXT_ROW[dz, 0], "text", TEXT_ROW[dz, 1], slots * ROWS, CORE)

    def both_x(self, name, dy, start):
        self.pass_image(name, XP, (0, dy), start, HALF)
        self.pass_image(name, XM, (0, dy), start, HALF)

    def both_y(self, name, dx, start):
        self.pass_image(name, YP, (dx, 0), start, HALF)
        self.pass_image(name, YM, (dx, 0), start, HALF)

    def onward_x(self, name, dy, start):
        self.pass_image(name, XP, (3, dy), start, QUAR)
        self.pass_image(name, XM, (1, dy), start + QUAR, QUAR)

    def onward_y(self, name, dx, start):
        self.pass_image(name, YP, (dx, 3), start, QUAR)
        self.pass_image(name, YM, (dx, 1), start + QUAR, QUAR)

    def ring(self, name, up, down, start):
        self.pass_text(name, ZP, up, start, HALF)
        self.pass_text(name, ZM, down, start, HALF)

    def gather(self):
        add, h1, h2 = self.add, 0, HALF
        add(X1, (), (), (self.both_x, X1, 0, h1))
        add(X2, (), (), (self.both_x, X2, 0, h2))
        add(Y1, (), (), (self.both_y, Y1, 0, h1))
        add(Y2, (), (), (self.both_y, Y2, 0, h2))
        add(XD, (X1,), (), (self.onward_x, XD, 0, h1))
        add(YD, (Y2,), (), (self.onward_y, YD, 0, h2))
        for d, far, near in ((3, X1, Y2), (1, X1, Y2), (2, XD, YD)):
            add(Y1S[d], (far,), (), (self.both_y, Y1S[d], d, h1))
            add(X2S[d], (near,), (), (self.both_x, X2S[d], d, h2))
        for d, group in enumerate((LA, LB, LB, LA)):
            add(LY[d], (Y1S[d],), (), (self.onward_y, group, d, h1))
            add(LX[d], (X2S[d],), (), (self.onward_x, group, d, h2))
        add(ZA0, (), (), (self.ring, ZA0, 0, 0, 0))
        add(ZB0, (), (), (self.ring, ZB0, 0, 0, HALF))
        add(ZA1, (ZA0,), (), (self.ring, ZA1, 7, 1, 0))
        add(ZB1, (ZB0,), (), (self.ring, ZB1, 7, 1, HALF))
        add(ZA2, (ZA1,), (), (self.ring, ZA2, 6, 2, 0))
        add(ZB2, (ZB1,), (), (self.ring, ZB2, 6, 2, HALF))
        add(ZC, (ZA1,), (), (self.pass_text, Z4, ZP2, 6, 0, HALF))
        add(ZD, (ZB1,), (), (self.pass_text, Z4, ZM2, 2, HALF, HALF))
        add(T0, (), (), (self.share, T0, 0, 1))
        add(T1, (ZA0, ZB0), (), (self.share, T1, 1, 2))
        add(T2, (ZA1, ZB1), (), (self.share, T2, 2, 2))
        add(T3, (ZA2, ZB2), (), (self.share, T3, 3, 2))
        add(T4, (Z4,), (ZC, ZD), (self.share, T4, 4, 1))

    def compute(self):
        run = self.run
        images = (
            (LA, LB, X2_2, Y1_2),
            (Y1_2, XD, YD, LA, Y1_1, X2_1),
            (Y1_3, Y1_1, X2_1, X2_3, Y1, Y2),
            (X1, X2, Y1, Y2),
        )
        texts = (
            (OH, COH, OWN_HI, (ZA1, ZB1, ZA2, ZB2, Z4)),
            (OL, COL, OWN_LO, (ZA0, ZB0, ZA1, ZB1)),
            (PH, CPH, OTHER_HI, (T2, T3, T4)),
            (PL, CPL, OTHER_LO, (T0, T1, T2)),
        )
        sent = {LA: (LY0, LX0, LY3, LX3), LB: (LY1, LX1, LY2, LX2), Z4: (ZC, ZD)}
        for block, here in enumerate(images):
            for _, coefs, start, there in texts:
                waits = here + there
                needs = sum((sent.get(wait, (wait,)) for wait in waits), ())
                self.add(coefs[block], waits, needs, (run.coef, block, start))
        for block in range(4):
            self.add(I[block], (), (COH[block], COL[block], CPH[block], CPL[block]), (run.images, block))
        for name, coefs, start, _ in texts:
            self.add(name, (), coefs, (run.texts, start))

    def ship(self, name, key, to_key, start, count, step):
        at = self.staged
        self.staged += count
        self.run.stage(key[0], self.row(key), self.parts.get(key, ()), start, count, at)
        self.run.copy(name, 1, "out", at, "in", at, count, step)
        self.coming.setdefault(name, []).append((to_key, start, count, at))

    def row(self, key):
        return IMAGE_ROW[key[1]] if key[0] == "image" else TEXT_ROW[key[1]]

    def ship_image(self, name, step, slot, start, count):
        to = ((slot[0] - step[0]) % NX, (slot[1] - step[1]) % NY)
        self.ship(name, ("image", slot), ("image", to), start, count, step)

    def ship_text(self, name, step, dz, start, count):
        self.ship(name, ("text", (dz, 0)), ("text", ((dz - step[2]) % NZ, 0)), start, count, step)

    def swap(self, name, first, slots):
        start, count = TEXT_ROW[first, 1], slots * ROWS
        at = start - NTH
        self.run.stage("text", start, (), 0, count, at)
        self.run.copy(name, 1, "out", at, "in", at, count, CORE)
        self.coming[name] = [
            (("text", (dz, 0)), 0, ROWS, TEXT_ROW[dz, 0]) for dz in TEXT_ORDER if at <= TEXT_ROW[dz, 0] < at + count
        ]

    def far_x(self, name, dy, start):
        self.ship_image(name, XM, (2, dy), start, QUAR)
        self.ship_image(name, XP, (2, dy), start + QUAR, QUAR)

    def far_y(self, name, dx, start):
        self.ship_image(name, YM, (dx, 2), start, QUAR)
        self.ship_image(name, YP, (dx, 2), start + QUAR, QUAR)

    def near_x(self, name, dy, start):
        self.ship_image(name, XM, (3, dy), start, HALF)
        self.ship_image(name, XP, (1, dy), start, HALF)

    def near_y(self, name, dx, start):
        self.ship_image(name, YM, (dx, 3), start, HALF)
        self.ship_image(name, YP, (dx, 1), start, HALF)

    def ring_back(self, name, up, down, start):
        self.ship_text(name, ZP, up, start, HALF)
        self.ship_text(name, ZM, down, start, HALF)

    def reduce(self):
        add, run, h1, h2 = self.add, self.run, 0, HALF

        def blocks(*slots):
            return tuple(sorted({I[IMAGE_ROW[slot] // BLOCK] for slot in slots}))

        for d in range(4):
            add(FY[d], (), blocks((d, 2)), (self.far_y, FY[d], d, h1))
            add(FX[d], (), blocks((2, d)), (self.far_x, FX[d], d, h2))
            add(NY_[d], (FY[d],), (FY[d],) + blocks((d, 3), (d, 1)), (self.near_y, NY_[d], d, h1))
            add(NX_[d], (FX[d],), (FX[d],) + blocks((3, d), (1, d)), (self.near_x, NX_[d], d, h2))
        add(GX, (NY2,), (NY2,) + blocks((2, 0)), (self.far_x, GX, 0, h1))
        add(GY, (NX2,), (NX2,) + blocks((0, 2)), (self.far_y, GY, 0, h2))
        add(KX, (NY1, NY3, GX), (NY1, NY3, GX) + blocks((3, 0), (1, 0)), (self.near_x, KX, 0, h1))
        add(KY, (NX1, NX3, GY), (NX1, NX3, GY) + blocks((0, 3), (0, 1)), (self.near_y, KY, 0, h2))
        add(S0, (), (PH,), (self.swap, S0, 4, 4))
        add(S1, (), (PL,), (self.swap, S1, 6, 4))
        add(RC, (S0,), (S0, OH), (self.ship_text, RC, ZP2, 4, 0, HALF))
        add(RD, (S0,), (S0, OH), (self.ship_text, RD, ZM2, 4, HALF, HALF))
        add(RA3, (S0,), (S0, OH), (self.ring_back, RA3, 3, 5, 0))
        add(RB3, (S0,), (S0, OH), (self.ring_back, RB3, 3, 5, HALF))
        add(RA2, (S0, S1, RC, RA3), (S1, RC, RA3, OL), (self.ring_back, RA2, 2, 6, 0))
        add(RB2, (S0, S1, RD, RB3), (S1, RD, RB3, OL), (self.ring_back, RB2, 2, 6, HALF))
        add(RA1, (RA2,), (RA2,), (self.ring_back, RA1, 1, 7, 0))
        add(RB1, (RB2,), (RB2,), (self.ring_back, RB1, 1, 7, HALF))
        add(END_IMAGE, (KX, KY, NY0, NX0), (KX, KY, NY0, NX0, I3), (self.finish, "image", (0, 0)))
        add(END_TEXT, (RA1, RB1), (RA1, RB1), (self.finish, "text", (0, 0)))

    def finish(self, kind, slot):
        self.run.finish(kind, self.row((kind, slot)), self.parts[kind, slot])


def position():
    blk = lax.axis_index("blk")
    row = lax.axis_index("row")
    return (blk // 2) % NX, (blk // (2 * NX)) * 2 + row // NZ, row % NZ, blk % 2


def device(here, step):
    x = (here[0] + step[0] + NX) % NX
    y = (here[1] + step[1] + NY) % NY
    z = (here[2] + step[2] + NZ) % NZ
    core = (here[3] + step[3]) % 2
    return (((y // 2) * NX + x) * 2 + core, (y % 2) * NZ + z)


def unit_of(values):
    norm_rows = jnp.sqrt(jnp.sum(values * values, axis=1, keepdims=True) + EPS)
    return values / norm_rows, norm_rows


def project_back(grad_hat, unit_rows, norm_rows):
    return (grad_hat - unit_rows * jnp.sum(unit_rows * grad_hat, axis=1, keepdims=True)) / norm_rows


def kernel(
    images, texts, scale, bias, image_hat_grad, text_hat_grad,
    image_hat, text_hat, image_acc, text_acc, coef, out_stage, in_stage, send_sem, recv_sem,
):
    here = position()
    barrier = pltpu.get_barrier_semaphore()
    for step in PARTNERS:
        pl.semaphore_signal(barrier, inc=1, device_id=device(here, step), device_id_type=MESH)
    scale_value = scale[0]
    bias_value = bias[0]
    buffers = {"image": image_hat, "text": text_hat, "out": out_stage, "in": in_stage}
    sums = {"image": image_acc, "text": text_acc}
    grads = {"image": image_hat_grad, "text": text_hat_grad}

    class Run:
        def __init__(self):
            self.rows = {}
            self.index = {}
            self.sent = [0, 0]

        def copy(self, name, phase, source, row, target, to_row, count, step):
            self.rows[name] = self.rows.get(name, 0) + count
            self.sent[phase] += count
            pltpu.make_async_remote_copy(
                src_ref=buffers[source].at[pl.ds(row, count)],
                dst_ref=buffers[target].at[pl.ds(to_row, count)],
                send_sem=send_sem.at[phase],
                recv_sem=recv_sem.at[self.index.setdefault(name, len(self.index))],
                device_id=device(here, step),
                device_id_type=MESH,
            ).start()

        def whole(self, rows, phase, name):
            return pltpu.make_async_remote_copy(
                src_ref=out_stage.at[pl.ds(0, rows)],
                dst_ref=in_stage.at[pl.ds(0, rows)],
                send_sem=send_sem.at[phase],
                recv_sem=recv_sem.at[self.index[name]],
                device_id=device(here, CORE),
                device_id_type=MESH,
            )

        def wait(self, *names):
            for name in names:
                self.whole(self.rows[name], 0, name).wait_recv()

        def wait_sent(self):
            for phase, rows in enumerate(self.sent):
                if rows:
                    self.whole(rows, phase, X1).wait_send()

        def coef(self, block, start):
            rows, cols = pl.ds(block * BLOCK, BLOCK), pl.ds(start, BLOCK)
            dots = lax.dot_general(image_hat[rows], text_hat[cols], NT, preferred_element_type=F32)
            logits = scale_value * dots + bias_value
            coef[rows, cols] = (scale_value * jax.nn.sigmoid(logits)).astype(BF16)
            top, left = OWN_IMAGE - block * BLOCK, OWN_TEXT - start
            if 0 <= top < BLOCK and 0 <= left < BLOCK:
                base = left // LANES * LANES
                pairs = logits[top : top + ROWS, base : base + LANES]
                row = lax.broadcasted_iota(jnp.int32, pairs.shape, 0)
                col = lax.broadcasted_iota(jnp.int32, pairs.shape, 1)
                sign = jnp.where(col - row == left - base, 1.0, -1.0).astype(F32)
                coef[pl.ds(OWN_IMAGE, ROWS), pl.ds(start + base, LANES)] = (
                    -scale_value * sign * jax.nn.sigmoid(-sign * pairs)
                ).astype(BF16)

        def images(self, block):
            rows = pl.ds(block * BLOCK, BLOCK)
            image_acc[rows] = lax.dot_general(coef[rows], text_hat[...], NN, preferred_element_type=F32)

        def texts(self, start):
            rows = pl.ds(start, BLOCK)
            text_acc[rows] = lax.dot_general(coef[:, rows], image_hat[...], TN, preferred_element_type=F32)

        def total(self, kind, row, parts, first, count):
            value = sums[kind][pl.ds(row + first, count)]
            for begin, size, at in parts:
                if begin <= first and first + count <= begin + size:
                    value = value + in_stage[pl.ds(at + first - begin, count)].astype(F32)
            return value

        def stage(self, kind, row, parts, start, count, at):
            step = QUAR if parts else min(count, ROWS)
            for first in range(start, start + count, step):
                value = self.total(kind, row, parts, first, step)
                out_stage[pl.ds(at + first - start, step)] = value.astype(BF16)

        def finish(self, kind, row, parts):
            for first in (0, HALF):
                grads[kind][pl.ds(first, HALF)] = self.total(kind, row, parts, first, HALF)

    run = Run()
    plan = Plan(run)
    image_hat[pl.ds(OWN_IMAGE, ROWS)] = unit_of(images[...])[0].astype(BF16)
    text_hat[pl.ds(OWN_TEXT, ROWS)] = unit_of(texts[...])[0].astype(BF16)
    pl.semaphore_wait(barrier, len(PARTNERS))
    plan.execute(ORDER)
    run.wait_sent()


def body(images, texts, scale, bias):
    width = images.shape[1]
    vmem = pl.BlockSpec(memory_space=pltpu.VMEM)
    smem = pl.BlockSpec(memory_space=pltpu.SMEM)
    shard = jax.ShapeDtypeStruct(images.shape, F32)
    image_hat_grad, text_hat_grad = pl.pallas_call(
        kernel,
        out_shape=(shard, shard),
        in_specs=[vmem, vmem, smem, smem],
        out_specs=(vmem, vmem),
        scratch_shapes=[
            pltpu.VMEM((NI, width), BF16),
            pltpu.VMEM((NTX, width), BF16),
            pltpu.VMEM((NI, width), F32),
            pltpu.VMEM((NTX, width), F32),
            pltpu.VMEM((NI, NTX), BF16),
            pltpu.VMEM((STAGE, width), BF16),
            pltpu.VMEM((STAGE, width), BF16),
            pltpu.SemaphoreType.DMA((2,)),
            pltpu.SemaphoreType.DMA((GROUPS,)),
        ],
        compiler_params=pltpu.CompilerParams(
            collective_id=0, has_side_effects=True, vmem_limit_bytes=48 * 2**20
        ),
    )(images, texts, scale, bias)
    return project_back(image_hat_grad, *unit_of(images)), project_back(text_hat_grad, *unit_of(texts))


def solution(mesh):
    placed = (P(("blk", "row"), None), P(("blk", "row"), None), P(), P())
    return jax.shard_map(
        body,
        mesh=mesh,
        in_specs=placed,
        out_specs=(P(("blk", "row"), None), P(("blk", "row"), None)),
        check_vma=False,
    )
```

```python
import jax
import jax.numpy as jnp
from jax import lax
from jax.experimental import pallas as pl
from jax.experimental.pallas import tpu as pltpu
from jax.sharding import PartitionSpec as P

EPS = 1e-06
F32 = jnp.float32
BF16 = jnp.bfloat16
MESH = pl.DeviceIdType.MESH
NT = (((1,), (1,)), ((), ()))
NN = (((1,), (0,)), ((), ()))
TN = (((0,), (0,)), ((), ()))

NX, NY, NZ = 4, 4, 8
ROWS = 64
HALF = 32
QUAR = 16
BLOCK = 256
LANES = 128
XP, XM = (1, 0, 0, 0), (-1, 0, 0, 0)
YP, YM = (0, 1, 0, 0), (0, -1, 0, 0)
ZP, ZM, ZP2, ZM2 = (0, 0, 1, 0), (0, 0, -1, 0), (0, 0, 2, 0), (0, 0, -2, 0)
CORE = (0, 0, 0, 1)
PARTNERS = (XP, XM, YP, YM, ZP, ZM, ZP2, ZM2, CORE)

IMAGE_ORDER = (
    (2, 2), (1, 2), (3, 2), (2, 1),
    (2, 3), (2, 0), (0, 2), (1, 1),
    (3, 1), (1, 3), (3, 3), (0, 1),
    (0, 3), (1, 0), (3, 0), (0, 0),
)
IMAGE_ROW = {slot: i * ROWS for i, slot in enumerate(IMAGE_ORDER)}
TEXT_ORDER = (4, 3, 5, 2, 6, 1, 7, 0)
NI = len(IMAGE_ORDER) * ROWS
NTH = len(TEXT_ORDER) * ROWS
NTX = 2 * NTH
TEXT_ROW = {(dz, dc): dc * NTH + i * ROWS for i, dz in enumerate(TEXT_ORDER) for dc in range(2)}
OWN_HI, OWN_LO, OTHER_HI, OTHER_LO = 0, BLOCK, NTH, NTH + BLOCK
OWN_IMAGE, OWN_TEXT = IMAGE_ROW[0, 0], TEXT_ROW[0, 0]
STAGE = 2176
GROUPS = 56
(
    X1, X2, Y1, Y2, XD, YD, Y1_1, Y1_2, Y1_3, X2_1, X2_2, X2_3, LY0, LY1, LY2, LY3, LX0, LX1, LX2,
    LX3, ZA0, ZA1, ZA2, ZB0, ZB1, ZB2, ZC, ZD, T0, T1, T2, T3, T4, COH0, COH1, COH2, COH3, COL0, COL1,
    COL2, COL3, CPH0, CPH1, CPH2, CPH3, CPL0, CPL1, CPL2, CPL3, I0, I1, I2, I3, OH, OL, PH, PL, S0,
    S1, FX0, FX1, FX2, FX3, FY0, FY1, FY2, FY3, NX0, NX1, NX2, NX3, NY0, NY1, NY2, NY3, GX, GY, KX,
    KY, RA1, RA2, RA3, RB1, RB2, RB3, RC, RD, END_IMAGE, END_TEXT, LA, LB, Z4,
) = range(92)
Y1S, X2S = (Y1, Y1_1, Y1_2, Y1_3), (X2, X2_1, X2_2, X2_3)
LX, LY, I = (LX0, LX1, LX2, LX3), (LY0, LY1, LY2, LY3), (I0, I1, I2, I3)
FX, FY, NX_, NY_ = (FX0, FX1, FX2, FX3), (FY0, FY1, FY2, FY3), (NX0, NX1, NX2, NX3), (NY0, NY1, NY2, NY3)
COH, COL = (COH0, COH1, COH2, COH3), (COL0, COL1, COL2, COL3)
CPH, CPL = (CPH0, CPH1, CPH2, CPH3), (CPL0, CPL1, CPL2, CPL3)

ORDER = (
    ZB0, X1, Y2, X2, ZA0, Y1, ZB1, Y1_3, YD, Y1_1, XD, X2_3, ZA1, X2_1, T0, LX3, T1, ZB2, T2, X2_2, Y1_2,
    LY3, ZA2, LX1, ZD, ZC, COL3, LY0, LX0, CPL3, LY1, LX2, LY2, CPL1, COL1, T3, COL2, CPL2, T4, COH3,
    COH1, CPH0, CPH3, CPH2, CPH1, PH, S0, CPL0, COH2, COH0, COL0, I0, OH, RD, RB3, FY2, FX2, I1, FY1, FX0,
    RC, FX3, RA3, FY0, FY3, FX1, PL, OL, NX2, S1, NY2, I2, NX3, NY1, I3, NX1, NY3, RB2, GX, GY, RA2, NX0,
    NY0, RB1, KX, KY, RA1, END_IMAGE, END_TEXT,
)


class Plan:
    def __init__(self, run):
        self.run = run
        self.parts = {}
        self.coming = {}
        self.taken = set()
        self.staged = NTH
        self.steps = {}
        self.gather()
        self.compute()
        self.reduce()

    def add(self, name, after, needs, *actions):
        self.steps[name] = (after, needs, actions)

    def execute(self, order):
        done = set()
        for name in order:
            after, needs, actions = self.steps[name]
            assert done.issuperset(needs)
            self.take(after)
            for action, *args in actions:
                action(*args)
            done.add(name)

    def take(self, names):
        for name in names:
            if name not in self.taken:
                self.taken.add(name)
                self.run.wait(name)
                for key, start, count, at in self.coming.get(name, ()):
                    self.parts.setdefault(key, []).append((start, count, at))

    def pass_image(self, name, step, slot, start, count):
        to = ((slot[0] - step[0]) % NX, (slot[1] - step[1]) % NY)
        self.run.copy(name, 0, "image", IMAGE_ROW[slot] + start, "image", IMAGE_ROW[to] + start, count, step)

    def pass_text(self, name, step, dz, start, count):
        to = (dz - step[2]) % NZ
        self.run.copy(name, 0, "text", TEXT_ROW[dz, 0] + start, "text", TEXT_ROW[to, 0] + start, count, step)

    def share(self, name, dz, slots):
        self.run.copy(name, 0, "text", TEXT_ROW[dz, 0], "text", TEXT_ROW[dz, 1], slots * ROWS, CORE)

    def both_x(self, name, dy, start):
        self.pass_image(name, XP, (0, dy), start, HALF)
        self.pass_image(name, XM, (0, dy), start, HALF)

    def both_y(self, name, dx, start):
        self.pass_image(name, YP, (dx, 0), start, HALF)
        self.pass_image(name, YM, (dx, 0), start, HALF)

    def onward_x(self, name, dy, start):
        self.pass_image(name, XP, (3, dy), start, QUAR)
        self.pass_image(name, XM, (1, dy), start + QUAR, QUAR)

    def onward_y(self, name, dx, start):
        self.pass_image(name, YP, (dx, 3), start, QUAR)
        self.pass_image(name, YM, (dx, 1), start + QUAR, QUAR)

    def ring(self, name, up, down, start):
        self.pass_text(name, ZP, up, start, HALF)
        self.pass_text(name, ZM, down, start, HALF)

    def gather(self):
        add, h1, h2 = self.add, 0, HALF
        add(X1, (), (), (self.both_x, X1, 0, h1))
        add(X2, (), (), (self.both_x, X2, 0, h2))
        add(Y1, (), (), (self.both_y, Y1, 0, h1))
        add(Y2, (), (), (self.both_y, Y2, 0, h2))
        add(XD, (X1,), (), (self.onward_x, XD, 0, h1))
        add(YD, (Y2,), (), (self.onward_y, YD, 0, h2))
        for d, far, near in ((3, X1, Y2), (1, X1, Y2), (2, XD, YD)):
            add(Y1S[d], (far,), (), (self.both_y, Y1S[d], d, h1))
            add(X2S[d], (near,), (), (self.both_x, X2S[d], d, h2))
        for d, group in enumerate((LA, LB, LB, LA)):
            add(LY[d], (Y1S[d],), (), (self.onward_y, group, d, h1))
            add(LX[d], (X2S[d],), (), (self.onward_x, group, d, h2))
        add(ZA0, (), (), (self.ring, ZA0, 0, 0, 0))
        add(ZB0, (), (), (self.ring, ZB0, 0, 0, HALF))
        add(ZA1, (ZA0,), (), (self.ring, ZA1, 7, 1, 0))
        add(ZB1, (ZB0,), (), (self.ring, ZB1, 7, 1, HALF))
        add(ZA2, (ZA1,), (), (self.ring, ZA2, 6, 2, 0))
        add(ZB2, (ZB1,), (), (self.ring, ZB2, 6, 2, HALF))
        add(ZC, (ZA1,), (), (self.pass_text, Z4, ZP2, 6, 0, HALF))
        add(ZD, (ZB1,), (), (self.pass_text, Z4, ZM2, 2, HALF, HALF))
        add(T0, (), (), (self.share, T0, 0, 1))
        add(T1, (ZA0, ZB0), (), (self.share, T1, 1, 2))
        add(T2, (ZA1, ZB1), (), (self.share, T2, 2, 2))
        add(T3, (ZA2, ZB2), (), (self.share, T3, 3, 2))
        add(T4, (Z4,), (ZC, ZD), (self.share, T4, 4, 1))

    def compute(self):
        run = self.run
        images = (
            (LA, LB, X2_2, Y1_2),
            (Y1_2, XD, YD, LA, Y1_1, X2_1),
            (Y1_3, Y1_1, X2_1, X2_3, Y1, Y2),
            (X1, X2, Y1, Y2),
        )
        texts = (
            (OH, COH, OWN_HI, (ZA1, ZB1, ZA2, ZB2, Z4)),
            (OL, COL, OWN_LO, (ZA0, ZB0, ZA1, ZB1)),
            (PH, CPH, OTHER_HI, (T2, T3, T4)),
            (PL, CPL, OTHER_LO, (T0, T1, T2)),
        )
        sent = {LA: (LY0, LX0, LY3, LX3), LB: (LY1, LX1, LY2, LX2), Z4: (ZC, ZD)}
        for block, here in enumerate(images):
            for _, coefs, start, there in texts:
                waits = here + there
                needs = sum((sent.get(wait, (wait,)) for wait in waits), ())
                self.add(coefs[block], waits, needs, (run.coef, block, start))
        for block in range(4):
            self.add(I[block], (), (COH[block], COL[block], CPH[block], CPL[block]), (run.images, block))
        for name, coefs, start, _ in texts:
            self.add(name, (), coefs, (run.texts, start))

    def ship(self, name, key, to_key, start, count, step):
        at = self.staged
        self.staged += count
        self.run.stage(key[0], self.row(key), self.parts.get(key, ()), start, count, at)
        self.run.copy(name, 1, "out", at, "in", at, count, step)
        self.coming.setdefault(name, []).append((to_key, start, count, at))

    def row(self, key):
        return IMAGE_ROW[key[1]] if key[0] == "image" else TEXT_ROW[key[1]]

    def ship_image(self, name, step, slot, start, count):
        to = ((slot[0] - step[0]) % NX, (slot[1] - step[1]) % NY)
        self.ship(name, ("image", slot), ("image", to), start, count, step)

    def ship_text(self, name, step, dz, start, count):
        self.ship(name, ("text", (dz, 0)), ("text", ((dz - step[2]) % NZ, 0)), start, count, step)

    def swap(self, name, first, slots):
        start, count = TEXT_ROW[first, 1], slots * ROWS
        at = start - NTH
        self.run.stage("text", start, (), 0, count, at)
        self.run.copy(name, 1, "out", at, "in", at, count, CORE)
        self.coming[name] = [
            (("text", (dz, 0)), 0, ROWS, TEXT_ROW[dz, 0]) for dz in TEXT_ORDER if at <= TEXT_ROW[dz, 0] < at + count
        ]

    def far_x(self, name, dy, start):
        self.ship_image(name, XM, (2, dy), start, QUAR)
        self.ship_image(name, XP, (2, dy), start + QUAR, QUAR)

    def far_y(self, name, dx, start):
        self.ship_image(name, YM, (dx, 2), start, QUAR)
        self.ship_image(name, YP, (dx, 2), start + QUAR, QUAR)

    def near_x(self, name, dy, start):
        self.ship_image(name, XM, (3, dy), start, HALF)
        self.ship_image(name, XP, (1, dy), start, HALF)

    def near_y(self, name, dx, start):
        self.ship_image(name, YM, (dx, 3), start, HALF)
        self.ship_image(name, YP, (dx, 1), start, HALF)

    def ring_back(self, name, up, down, start):
        self.ship_text(name, ZP, up, start, HALF)
        self.ship_text(name, ZM, down, start, HALF)

    def reduce(self):
        add, run, h1, h2 = self.add, self.run, 0, HALF

        def blocks(*slots):
            return tuple(sorted({I[IMAGE_ROW[slot] // BLOCK] for slot in slots}))

        for d in range(4):
            add(FY[d], (), blocks((d, 2)), (self.far_y, FY[d], d, h1))
            add(FX[d], (), blocks((2, d)), (self.far_x, FX[d], d, h2))
            add(NY_[d], (FY[d],), (FY[d],) + blocks((d, 3), (d, 1)), (self.near_y, NY_[d], d, h1))
            add(NX_[d], (FX[d],), (FX[d],) + blocks((3, d), (1, d)), (self.near_x, NX_[d], d, h2))
        add(GX, (NY2,), (NY2,) + blocks((2, 0)), (self.far_x, GX, 0, h1))
        add(GY, (NX2,), (NX2,) + blocks((0, 2)), (self.far_y, GY, 0, h2))
        add(KX, (NY1, NY3, GX), (NY1, NY3, GX) + blocks((3, 0), (1, 0)), (self.near_x, KX, 0, h1))
        add(KY, (NX1, NX3, GY), (NX1, NX3, GY) + blocks((0, 3), (0, 1)), (self.near_y, KY, 0, h2))
        add(S0, (), (PH,), (self.swap, S0, 4, 4))
        add(S1, (), (PL,), (self.swap, S1, 6, 4))
        add(RC, (S0,), (S0, OH), (self.ship_text, RC, ZP2, 4, 0, HALF))
        add(RD, (S0,), (S0, OH), (self.ship_text, RD, ZM2, 4, HALF, HALF))
        add(RA3, (S0,), (S0, OH), (self.ring_back, RA3, 3, 5, 0))
        add(RB3, (S0,), (S0, OH), (self.ring_back, RB3, 3, 5, HALF))
        add(RA2, (S0, S1, RC, RA3), (S1, RC, RA3, OL), (self.ring_back, RA2, 2, 6, 0))
        add(RB2, (S0, S1, RD, RB3), (S1, RD, RB3, OL), (self.ring_back, RB2, 2, 6, HALF))
        add(RA1, (RA2,), (RA2,), (self.ring_back, RA1, 1, 7, 0))
        add(RB1, (RB2,), (RB2,), (self.ring_back, RB1, 1, 7, HALF))
        add(END_IMAGE, (KX, KY, NY0, NX0), (KX, KY, NY0, NX0, I3), (self.finish, "image", (0, 0)))
        add(END_TEXT, (RA1, RB1), (RA1, RB1), (self.finish, "text", (0, 0)))

    def finish(self, kind, slot):
        self.run.finish(kind, self.row((kind, slot)), self.parts[kind, slot])


def position():
    blk = lax.axis_index("blk")
    row = lax.axis_index("row")
    return (blk // 2) % NX, (blk // (2 * NX)) * 2 + row // NZ, row % NZ, blk % 2


def device(here, step):
    x = (here[0] + step[0] + NX) % NX
    y = (here[1] + step[1] + NY) % NY
    z = (here[2] + step[2] + NZ) % NZ
    core = (here[3] + step[3]) % 2
    return (((y // 2) * NX + x) * 2 + core, (y % 2) * NZ + z)


def norm_of(values):
    return jnp.sqrt(jnp.sum(values * values, axis=1, keepdims=True) + EPS)


def kernel(
    images, texts, scale, bias, image_part, text_part,
    image_hat, text_hat, image_acc, text_acc, coef, out_stage, in_stage,
    image_unit, text_unit, send_sem, recv_sem,
):
    here = position()
    barrier = pltpu.get_barrier_semaphore()
    for step in PARTNERS:
        pl.semaphore_signal(barrier, inc=1, device_id=device(here, step), device_id_type=MESH)
    scale_value = scale[0]
    bias_value = bias[0]
    buffers = {"image": image_hat, "text": text_hat, "out": out_stage, "in": in_stage}
    sums = {"image": image_acc, "text": text_acc}
    units = {"image": image_unit, "text": text_unit}
    grads = {"image": image_part, "text": text_part}

    class Run:
        def __init__(self):
            self.rows = {}
            self.index = {}
            self.sent = [0, 0]

        def copy(self, name, phase, source, row, target, to_row, count, step):
            self.rows[name] = self.rows.get(name, 0) + count
            self.sent[phase] += count
            pltpu.make_async_remote_copy(
                src_ref=buffers[source].at[pl.ds(row, count)],
                dst_ref=buffers[target].at[pl.ds(to_row, count)],
                send_sem=send_sem.at[phase],
                recv_sem=recv_sem.at[self.index.setdefault(name, len(self.index))],
                device_id=device(here, step),
                device_id_type=MESH,
            ).start()

        def whole(self, rows, phase, name):
            return pltpu.make_async_remote_copy(
                src_ref=out_stage.at[pl.ds(0, rows)],
                dst_ref=in_stage.at[pl.ds(0, rows)],
                send_sem=send_sem.at[phase],
                recv_sem=recv_sem.at[self.index[name]],
                device_id=device(here, CORE),
                device_id_type=MESH,
            )

        def wait(self, *names):
            for name in names:
                self.whole(self.rows[name], 0, name).wait_recv()

        def wait_sent(self):
            for phase, rows in enumerate(self.sent):
                if rows:
                    self.whole(rows, phase, X1).wait_send()

        def coef(self, block, start):
            rows, cols = pl.ds(block * BLOCK, BLOCK), pl.ds(start, BLOCK)
            dots = lax.dot_general(image_hat[rows], text_hat[cols], NT, preferred_element_type=F32)
            logits = scale_value * dots + bias_value
            coef[rows, cols] = (scale_value * jax.nn.sigmoid(logits)).astype(BF16)
            top, left = OWN_IMAGE - block * BLOCK, OWN_TEXT - start
            if 0 <= top < BLOCK and 0 <= left < BLOCK:
                base = left // LANES * LANES
                pairs = logits[top : top + ROWS, base : base + LANES]
                row = lax.broadcasted_iota(jnp.int32, pairs.shape, 0)
                col = lax.broadcasted_iota(jnp.int32, pairs.shape, 1)
                sign = jnp.where(col - row == left - base, 1.0, -1.0).astype(F32)
                coef[pl.ds(OWN_IMAGE, ROWS), pl.ds(start + base, LANES)] = (
                    -scale_value * sign * jax.nn.sigmoid(-sign * pairs)
                ).astype(BF16)

        def images(self, block):
            rows = pl.ds(block * BLOCK, BLOCK)
            image_acc[rows] = lax.dot_general(coef[rows], text_hat[...], NN, preferred_element_type=F32)

        def texts(self, start):
            rows = pl.ds(start, BLOCK)
            text_acc[rows] = lax.dot_general(coef[:, rows], image_hat[...], TN, preferred_element_type=F32)

        def total(self, kind, row, parts, first, count):
            value = sums[kind][pl.ds(row + first, count)]
            for begin, size, at in parts:
                if begin <= first and first + count <= begin + size:
                    value = value + in_stage[pl.ds(at + first - begin, count)].astype(F32)
            return value

        def stage(self, kind, row, parts, start, count, at):
            step = QUAR if parts else min(count, ROWS)
            for first in range(start, start + count, step):
                value = self.total(kind, row, parts, first, step)
                out_stage[pl.ds(at + first - start, step)] = value.astype(BF16)

        def finish(self, kind, row, parts):
            for first in (0, HALF):
                rows = pl.ds(first, HALF)
                value, unit = self.total(kind, row, parts, first, HALF), units[kind][rows]
                grads[kind][rows] = value - unit * jnp.sum(unit * value, axis=1, keepdims=True)

    run = Run()
    plan = Plan(run)
    image_unit[...] = images[...] / norm_of(images[...])
    image_hat[pl.ds(OWN_IMAGE, ROWS)] = image_unit[...].astype(BF16)
    text_unit[...] = texts[...] / norm_of(texts[...])
    text_hat[pl.ds(OWN_TEXT, ROWS)] = text_unit[...].astype(BF16)
    pl.semaphore_wait(barrier, len(PARTNERS))
    plan.execute(ORDER)
    run.wait_sent()


def body(images, texts, scale, bias):
    width = images.shape[1]
    vmem = pl.BlockSpec(memory_space=pltpu.VMEM)
    smem = pl.BlockSpec(memory_space=pltpu.SMEM)
    shard = jax.ShapeDtypeStruct(images.shape, F32)
    image_part, text_part = pl.pallas_call(
        kernel,
        out_shape=(shard, shard),
        in_specs=[vmem, vmem, smem, smem],
        out_specs=(vmem, vmem),
        scratch_shapes=[
            pltpu.VMEM((NI, width), BF16),
            pltpu.VMEM((NTX, width), BF16),
            pltpu.VMEM((NI, width), F32),
            pltpu.VMEM((NTX, width), F32),
            pltpu.VMEM((NI, NTX), BF16),
            pltpu.VMEM((STAGE, width), BF16),
            pltpu.VMEM((STAGE, width), BF16),
            pltpu.VMEM((ROWS, width), F32),
            pltpu.VMEM((ROWS, width), F32),
            pltpu.SemaphoreType.DMA((2,)),
            pltpu.SemaphoreType.DMA((GROUPS,)),
        ],
        compiler_params=pltpu.CompilerParams(
            collective_id=0, has_side_effects=True, vmem_limit_bytes=48 * 2**20
        ),
    )(images, texts, scale, bias)
    return image_part / norm_of(images), text_part / norm_of(texts)


def solution(mesh):
    placed = (P(("blk", "row"), None), P(("blk", "row"), None), P(), P())
    return jax.shard_map(
        body,
        mesh=mesh,
        in_specs=placed,
        out_specs=(P(("blk", "row"), None), P(("blk", "row"), None)),
        check_vma=False,
    )
```

```python
import jax
import jax.numpy as jnp
from jax import lax
from jax.experimental import pallas as pl
from jax.experimental.pallas import tpu as pltpu
from jax.sharding import PartitionSpec as P

EPS = 1e-06
F32 = jnp.float32
BF16 = jnp.bfloat16
MESH = pl.DeviceIdType.MESH
NT = (((1,), (1,)), ((), ()))
NN = (((1,), (0,)), ((), ()))
TN = (((0,), (0,)), ((), ()))

NX, NY, NZ = 4, 4, 8
ROWS = 64
HALF = 32
QUAR = 16
BLOCK = 256
LANES = 128
XP, XM = (1, 0, 0, 0), (-1, 0, 0, 0)
YP, YM = (0, 1, 0, 0), (0, -1, 0, 0)
ZP, ZM, ZP2, ZM2 = (0, 0, 1, 0), (0, 0, -1, 0), (0, 0, 2, 0), (0, 0, -2, 0)
CORE = (0, 0, 0, 1)
PARTNERS = (XP, XM, YP, YM, ZP, ZM, ZP2, ZM2, CORE)

IMAGE_ORDER = (
    (2, 2), (1, 2), (3, 2), (2, 1),
    (2, 3), (2, 0), (0, 2), (1, 1),
    (3, 1), (1, 3), (3, 3), (0, 1),
    (0, 3), (1, 0), (3, 0), (0, 0),
)
IMAGE_ROW = {slot: i * ROWS for i, slot in enumerate(IMAGE_ORDER)}
TEXT_ORDER = (4, 3, 5, 2, 6, 1, 7, 0)
NI = len(IMAGE_ORDER) * ROWS
NTH = len(TEXT_ORDER) * ROWS
NTX = 2 * NTH
TEXT_ROW = {(dz, dc): dc * NTH + i * ROWS for i, dz in enumerate(TEXT_ORDER) for dc in range(2)}
OWN_HI, OWN_LO, OTHER_HI, OTHER_LO = 0, BLOCK, NTH, NTH + BLOCK
OWN_IMAGE, OWN_TEXT = IMAGE_ROW[0, 0], TEXT_ROW[0, 0]
STAGE = 2176
GROUPS = 56
(
    X1, X2, Y1, Y2, XD, YD, Y1_1, Y1_2, Y1_3, X2_1, X2_2, X2_3, LY0, LY1, LY2, LY3, LX0, LX1, LX2,
    LX3, ZA0, ZA1, ZA2, ZB0, ZB1, ZB2, ZC, ZD, T0, T1, T2, T3, T4, COH0, COH1, COH2, COH3, COL0, COL1,
    COL2, COL3, CPH0, CPH1, CPH2, CPH3, CPL0, CPL1, CPL2, CPL3, I0, I1, I2, I3, OH, OL, PH, PL, S0,
    S1, FX0, FX1, FX2, FX3, FY0, FY1, FY2, FY3, NX0, NX1, NX2, NX3, NY0, NY1, NY2, NY3, GX, GY, KX,
    KY, RA1, RA2, RA3, RB1, RB2, RB3, RC, RD, END_IMAGE, END_TEXT, LA, LB, Z4,
    NORM_IMAGES, NORM_TEXTS,
) = range(94)
Y1S, X2S = (Y1, Y1_1, Y1_2, Y1_3), (X2, X2_1, X2_2, X2_3)
LX, LY, I = (LX0, LX1, LX2, LX3), (LY0, LY1, LY2, LY3), (I0, I1, I2, I3)
FX, FY, NX_, NY_ = (FX0, FX1, FX2, FX3), (FY0, FY1, FY2, FY3), (NX0, NX1, NX2, NX3), (NY0, NY1, NY2, NY3)
COH, COL = (COH0, COH1, COH2, COH3), (COL0, COL1, COL2, COL3)
CPH, CPL = (CPH0, CPH1, CPH2, CPH3), (CPL0, CPL1, CPL2, CPL3)

ORDER = (
    NORM_IMAGES, X1, Y2, X2, Y1, NORM_TEXTS, ZB0, ZA0, ZB1, Y1_3, YD, Y1_1, XD, X2_3, ZA1, X2_1, T0, LX3,
    T1, ZB2, T2, X2_2, Y1_2, LY3, ZA2, LX1, ZD, ZC, COL3, LY0, LX0, CPL3, LY1, LX2, LY2, CPL1, COL1, T3,
    COL2, CPL2, T4, COH3, COH1, CPH0, CPH3, CPH2, CPH1, PH, S0, CPL0, COH2, COH0, COL0, I0, OH, RD, RB3,
    FY2, FX2, I1, FY1, FX0, RC, FX3, RA3, FY0, FY3, FX1, PL, OL, NX2, S1, NY2, I2, NX3, NY1, I3, NX1, NY3,
    RB2, GX, GY, RA2, NX0, NY0, RB1, KX, KY, RA1, END_IMAGE, END_TEXT,
)


class Plan:
    def __init__(self, run):
        self.run = run
        self.parts = {}
        self.coming = {}
        self.taken = set()
        self.staged = NTH
        self.steps = {}
        self.gather()
        self.compute()
        self.reduce()

    def add(self, name, after, needs, *actions):
        self.steps[name] = (after, needs, actions)

    def execute(self, order):
        done = set()
        for name in order:
            after, needs, actions = self.steps[name]
            assert done.issuperset(needs)
            self.take(after)
            for action, *args in actions:
                action(*args)
            done.add(name)

    def take(self, names):
        for name in names:
            if name not in self.taken:
                self.taken.add(name)
                self.run.wait(name)
                for key, start, count, at in self.coming.get(name, ()):
                    self.parts.setdefault(key, []).append((start, count, at))

    def pass_image(self, name, step, slot, start, count):
        to = ((slot[0] - step[0]) % NX, (slot[1] - step[1]) % NY)
        self.run.copy(name, 0, "image", IMAGE_ROW[slot] + start, "image", IMAGE_ROW[to] + start, count, step)

    def pass_text(self, name, step, dz, start, count):
        to = (dz - step[2]) % NZ
        self.run.copy(name, 0, "text", TEXT_ROW[dz, 0] + start, "text", TEXT_ROW[to, 0] + start, count, step)

    def share(self, name, dz, slots):
        self.run.copy(name, 0, "text", TEXT_ROW[dz, 0], "text", TEXT_ROW[dz, 1], slots * ROWS, CORE)

    def both_x(self, name, dy, start):
        self.pass_image(name, XP, (0, dy), start, HALF)
        self.pass_image(name, XM, (0, dy), start, HALF)

    def both_y(self, name, dx, start):
        self.pass_image(name, YP, (dx, 0), start, HALF)
        self.pass_image(name, YM, (dx, 0), start, HALF)

    def onward_x(self, name, dy, start):
        self.pass_image(name, XP, (3, dy), start, QUAR)
        self.pass_image(name, XM, (1, dy), start + QUAR, QUAR)

    def onward_y(self, name, dx, start):
        self.pass_image(name, YP, (dx, 3), start, QUAR)
        self.pass_image(name, YM, (dx, 1), start + QUAR, QUAR)

    def ring(self, name, up, down, start):
        self.pass_text(name, ZP, up, start, HALF)
        self.pass_text(name, ZM, down, start, HALF)

    def gather(self):
        add, h1, h2 = self.add, 0, HALF
        add(NORM_IMAGES, (), (), (self.run.normalize, "image", OWN_IMAGE))
        add(NORM_TEXTS, (), (), (self.run.normalize, "text", OWN_TEXT))
        add(X1, (), (NORM_IMAGES,), (self.both_x, X1, 0, h1))
        add(X2, (), (NORM_IMAGES,), (self.both_x, X2, 0, h2))
        add(Y1, (), (NORM_IMAGES,), (self.both_y, Y1, 0, h1))
        add(Y2, (), (NORM_IMAGES,), (self.both_y, Y2, 0, h2))
        add(XD, (X1,), (), (self.onward_x, XD, 0, h1))
        add(YD, (Y2,), (), (self.onward_y, YD, 0, h2))
        for d, far, near in ((3, X1, Y2), (1, X1, Y2), (2, XD, YD)):
            add(Y1S[d], (far,), (), (self.both_y, Y1S[d], d, h1))
            add(X2S[d], (near,), (), (self.both_x, X2S[d], d, h2))
        for d, group in enumerate((LA, LB, LB, LA)):
            add(LY[d], (Y1S[d],), (), (self.onward_y, group, d, h1))
            add(LX[d], (X2S[d],), (), (self.onward_x, group, d, h2))
        add(ZA0, (), (NORM_TEXTS,), (self.ring, ZA0, 0, 0, 0))
        add(ZB0, (), (NORM_TEXTS,), (self.ring, ZB0, 0, 0, HALF))
        add(ZA1, (ZA0,), (), (self.ring, ZA1, 7, 1, 0))
        add(ZB1, (ZB0,), (), (self.ring, ZB1, 7, 1, HALF))
        add(ZA2, (ZA1,), (), (self.ring, ZA2, 6, 2, 0))
        add(ZB2, (ZB1,), (), (self.ring, ZB2, 6, 2, HALF))
        add(ZC, (ZA1,), (), (self.pass_text, Z4, ZP2, 6, 0, HALF))
        add(ZD, (ZB1,), (), (self.pass_text, Z4, ZM2, 2, HALF, HALF))
        add(T0, (), (NORM_TEXTS,), (self.share, T0, 0, 1))
        add(T1, (ZA0, ZB0), (), (self.share, T1, 1, 2))
        add(T2, (ZA1, ZB1), (), (self.share, T2, 2, 2))
        add(T3, (ZA2, ZB2), (), (self.share, T3, 3, 2))
        add(T4, (Z4,), (ZC, ZD), (self.share, T4, 4, 1))

    def compute(self):
        run = self.run
        images = (
            (LA, LB, X2_2, Y1_2),
            (Y1_2, XD, YD, LA, Y1_1, X2_1),
            (Y1_3, Y1_1, X2_1, X2_3, Y1, Y2),
            (X1, X2, Y1, Y2),
        )
        texts = (
            (OH, COH, OWN_HI, (ZA1, ZB1, ZA2, ZB2, Z4)),
            (OL, COL, OWN_LO, (ZA0, ZB0, ZA1, ZB1)),
            (PH, CPH, OTHER_HI, (T2, T3, T4)),
            (PL, CPL, OTHER_LO, (T0, T1, T2)),
        )
        sent = {LA: (LY0, LX0, LY3, LX3), LB: (LY1, LX1, LY2, LX2), Z4: (ZC, ZD)}
        for block, here in enumerate(images):
            for _, coefs, start, there in texts:
                waits = here + there
                needs = sum((sent.get(wait, (wait,)) for wait in waits), ())
                self.add(coefs[block], waits, needs, (run.coef, block, start))
        for block in range(4):
            self.add(I[block], (), (COH[block], COL[block], CPH[block], CPL[block]), (run.images, block))
        for name, coefs, start, _ in texts:
            self.add(name, (), coefs, (run.texts, start))

    def ship(self, name, key, to_key, start, count, step):
        at = self.staged
        self.staged += count
        self.run.stage(key[0], self.row(key), self.parts.get(key, ()), start, count, at)
        self.run.copy(name, 1, "out", at, "in", at, count, step)
        self.coming.setdefault(name, []).append((to_key, start, count, at))

    def row(self, key):
        return IMAGE_ROW[key[1]] if key[0] == "image" else TEXT_ROW[key[1]]

    def ship_image(self, name, step, slot, start, count):
        to = ((slot[0] - step[0]) % NX, (slot[1] - step[1]) % NY)
        self.ship(name, ("image", slot), ("image", to), start, count, step)

    def ship_text(self, name, step, dz, start, count):
        self.ship(name, ("text", (dz, 0)), ("text", ((dz - step[2]) % NZ, 0)), start, count, step)

    def swap(self, name, first, slots):
        start, count = TEXT_ROW[first, 1], slots * ROWS
        at = start - NTH
        self.run.stage("text", start, (), 0, count, at)
        self.run.copy(name, 1, "out", at, "in", at, count, CORE)
        self.coming[name] = [
            (("text", (dz, 0)), 0, ROWS, TEXT_ROW[dz, 0]) for dz in TEXT_ORDER if at <= TEXT_ROW[dz, 0] < at + count
        ]

    def far_x(self, name, dy, start):
        self.ship_image(name, XM, (2, dy), start, QUAR)
        self.ship_image(name, XP, (2, dy), start + QUAR, QUAR)

    def far_y(self, name, dx, start):
        self.ship_image(name, YM, (dx, 2), start, QUAR)
        self.ship_image(name, YP, (dx, 2), start + QUAR, QUAR)

    def near_x(self, name, dy, start):
        self.ship_image(name, XM, (3, dy), start, HALF)
        self.ship_image(name, XP, (1, dy), start, HALF)

    def near_y(self, name, dx, start):
        self.ship_image(name, YM, (dx, 3), start, HALF)
        self.ship_image(name, YP, (dx, 1), start, HALF)

    def ring_back(self, name, up, down, start):
        self.ship_text(name, ZP, up, start, HALF)
        self.ship_text(name, ZM, down, start, HALF)

    def reduce(self):
        add, run, h1, h2 = self.add, self.run, 0, HALF

        def blocks(*slots):
            return tuple(sorted({I[IMAGE_ROW[slot] // BLOCK] for slot in slots}))

        for d in range(4):
            add(FY[d], (), blocks((d, 2)), (self.far_y, FY[d], d, h1))
            add(FX[d], (), blocks((2, d)), (self.far_x, FX[d], d, h2))
            add(NY_[d], (FY[d],), (FY[d],) + blocks((d, 3), (d, 1)), (self.near_y, NY_[d], d, h1))
            add(NX_[d], (FX[d],), (FX[d],) + blocks((3, d), (1, d)), (self.near_x, NX_[d], d, h2))
        add(GX, (NY2,), (NY2,) + blocks((2, 0)), (self.far_x, GX, 0, h1))
        add(GY, (NX2,), (NX2,) + blocks((0, 2)), (self.far_y, GY, 0, h2))
        add(KX, (NY1, NY3, GX), (NY1, NY3, GX) + blocks((3, 0), (1, 0)), (self.near_x, KX, 0, h1))
        add(KY, (NX1, NX3, GY), (NX1, NX3, GY) + blocks((0, 3), (0, 1)), (self.near_y, KY, 0, h2))
        add(S0, (), (PH,), (self.swap, S0, 4, 4))
        add(S1, (), (PL,), (self.swap, S1, 6, 4))
        add(RC, (S0,), (S0, OH), (self.ship_text, RC, ZP2, 4, 0, HALF))
        add(RD, (S0,), (S0, OH), (self.ship_text, RD, ZM2, 4, HALF, HALF))
        add(RA3, (S0,), (S0, OH), (self.ring_back, RA3, 3, 5, 0))
        add(RB3, (S0,), (S0, OH), (self.ring_back, RB3, 3, 5, HALF))
        add(RA2, (S0, S1, RC, RA3), (S1, RC, RA3, OL), (self.ring_back, RA2, 2, 6, 0))
        add(RB2, (S0, S1, RD, RB3), (S1, RD, RB3, OL), (self.ring_back, RB2, 2, 6, HALF))
        add(RA1, (RA2,), (RA2,), (self.ring_back, RA1, 1, 7, 0))
        add(RB1, (RB2,), (RB2,), (self.ring_back, RB1, 1, 7, HALF))
        add(END_IMAGE, (KX, KY, NY0, NX0), (KX, KY, NY0, NX0, I3), (self.finish, "image", (0, 0)))
        add(END_TEXT, (RA1, RB1), (RA1, RB1), (self.finish, "text", (0, 0)))

    def finish(self, kind, slot):
        self.run.finish(kind, self.row((kind, slot)), self.parts[kind, slot])


def position():
    blk = lax.axis_index("blk")
    row = lax.axis_index("row")
    return (blk // 2) % NX, (blk // (2 * NX)) * 2 + row // NZ, row % NZ, blk % 2


def device(here, step):
    x = (here[0] + step[0] + NX) % NX
    y = (here[1] + step[1] + NY) % NY
    z = (here[2] + step[2] + NZ) % NZ
    core = (here[3] + step[3]) % 2
    return (((y // 2) * NX + x) * 2 + core, (y % 2) * NZ + z)


def norm_of(values):
    return jnp.sqrt(jnp.sum(values * values, axis=1, keepdims=True) + EPS)


def kernel(
    images, texts, scale, bias, image_part, text_part,
    image_hat, text_hat, image_acc, text_acc, coef, out_stage, in_stage,
    image_unit, text_unit, send_sem, recv_sem,
):
    here = position()
    barrier = pltpu.get_barrier_semaphore()
    for step in PARTNERS:
        pl.semaphore_signal(barrier, inc=1, device_id=device(here, step), device_id_type=MESH)
    scale_value = scale[0]
    bias_value = bias[0]
    buffers = {"image": image_hat, "text": text_hat, "out": out_stage, "in": in_stage}
    sums = {"image": image_acc, "text": text_acc}
    raw = {"image": images, "text": texts}
    units = {"image": image_unit, "text": text_unit}
    grads = {"image": image_part, "text": text_part}

    class Run:
        def __init__(self):
            self.rows = {}
            self.index = {}
            self.sent = [0, 0]

        def normalize(self, kind, row):
            units[kind][...] = raw[kind][...] / norm_of(raw[kind][...])
            buffers[kind][pl.ds(row, ROWS)] = units[kind][...].astype(BF16)

        def copy(self, name, phase, source, row, target, to_row, count, step):
            self.rows[name] = self.rows.get(name, 0) + count
            self.sent[phase] += count
            pltpu.make_async_remote_copy(
                src_ref=buffers[source].at[pl.ds(row, count)],
                dst_ref=buffers[target].at[pl.ds(to_row, count)],
                send_sem=send_sem.at[phase],
                recv_sem=recv_sem.at[self.index.setdefault(name, len(self.index))],
                device_id=device(here, step),
                device_id_type=MESH,
            ).start()

        def whole(self, rows, phase, name):
            return pltpu.make_async_remote_copy(
                src_ref=out_stage.at[pl.ds(0, rows)],
                dst_ref=in_stage.at[pl.ds(0, rows)],
                send_sem=send_sem.at[phase],
                recv_sem=recv_sem.at[self.index[name]],
                device_id=device(here, CORE),
                device_id_type=MESH,
            )

        def wait(self, *names):
            for name in names:
                self.whole(self.rows[name], 0, name).wait_recv()

        def wait_sent(self):
            for phase, rows in enumerate(self.sent):
                if rows:
                    self.whole(rows, phase, X1).wait_send()

        def coef(self, block, start):
            rows, cols = pl.ds(block * BLOCK, BLOCK), pl.ds(start, BLOCK)
            dots = lax.dot_general(image_hat[rows], text_hat[cols], NT, preferred_element_type=F32)
            logits = scale_value * dots + bias_value
            coef[rows, cols] = (scale_value * jax.nn.sigmoid(logits)).astype(BF16)
            top, left = OWN_IMAGE - block * BLOCK, OWN_TEXT - start
            if 0 <= top < BLOCK and 0 <= left < BLOCK:
                base = left // LANES * LANES
                pairs = logits[top : top + ROWS, base : base + LANES]
                row = lax.broadcasted_iota(jnp.int32, pairs.shape, 0)
                col = lax.broadcasted_iota(jnp.int32, pairs.shape, 1)
                sign = jnp.where(col - row == left - base, 1.0, -1.0).astype(F32)
                coef[pl.ds(OWN_IMAGE, ROWS), pl.ds(start + base, LANES)] = (
                    -scale_value * sign * jax.nn.sigmoid(-sign * pairs)
                ).astype(BF16)

        def images(self, block):
            rows = pl.ds(block * BLOCK, BLOCK)
            image_acc[rows] = lax.dot_general(coef[rows], text_hat[...], NN, preferred_element_type=F32)

        def texts(self, start):
            rows = pl.ds(start, BLOCK)
            text_acc[rows] = lax.dot_general(coef[:, rows], image_hat[...], TN, preferred_element_type=F32)

        def total(self, kind, row, parts, first, count):
            value = sums[kind][pl.ds(row + first, count)]
            for begin, size, at in parts:
                if begin <= first and first + count <= begin + size:
                    value = value + in_stage[pl.ds(at + first - begin, count)].astype(F32)
            return value

        def stage(self, kind, row, parts, start, count, at):
            step = QUAR if parts else min(count, ROWS)
            for first in range(start, start + count, step):
                value = self.total(kind, row, parts, first, step)
                out_stage[pl.ds(at + first - start, step)] = value.astype(BF16)

        def finish(self, kind, row, parts):
            for first in (0, HALF):
                rows = pl.ds(first, HALF)
                value, unit = self.total(kind, row, parts, first, HALF), units[kind][rows]
                grads[kind][rows] = value - unit * jnp.sum(unit * value, axis=1, keepdims=True)

    run = Run()
    plan = Plan(run)
    pl.semaphore_wait(barrier, len(PARTNERS))
    plan.execute(ORDER)
    run.wait_sent()


def body(images, texts, scale, bias):
    width = images.shape[1]
    vmem = pl.BlockSpec(memory_space=pltpu.VMEM)
    smem = pl.BlockSpec(memory_space=pltpu.SMEM)
    shard = jax.ShapeDtypeStruct(images.shape, F32)
    image_part, text_part = pl.pallas_call(
        kernel,
        out_shape=(shard, shard),
        in_specs=[vmem, vmem, smem, smem],
        out_specs=(vmem, vmem),
        scratch_shapes=[
            pltpu.VMEM((NI, width), BF16),
            pltpu.VMEM((NTX, width), BF16),
            pltpu.VMEM((NI, width), F32),
            pltpu.VMEM((NTX, width), F32),
            pltpu.VMEM((NI, NTX), BF16),
            pltpu.VMEM((STAGE, width), BF16),
            pltpu.VMEM((STAGE, width), BF16),
            pltpu.VMEM((ROWS, width), F32),
            pltpu.VMEM((ROWS, width), F32),
            pltpu.SemaphoreType.DMA((2,)),
            pltpu.SemaphoreType.DMA((GROUPS,)),
        ],
        compiler_params=pltpu.CompilerParams(
            collective_id=0, has_side_effects=True, vmem_limit_bytes=48 * 2**20
        ),
    )(images, texts, scale, bias)
    return image_part / norm_of(images), text_part / norm_of(texts)


def solution(mesh):
    placed = (P(("blk", "row"), None), P(("blk", "row"), None), P(), P())
    return jax.shard_map(
        body,
        mesh=mesh,
        in_specs=placed,
        out_specs=(P(("blk", "row"), None), P(("blk", "row"), None)),
        check_vma=False,
    )
```
